32 devices in a mesh: groups: 2 (over x), tier: 16 (over z, y, core).
Axes of the slice: x: 2, y: 2, z: 4, core: 2. Of those that a mesh axis runs over, the one named last changes fastest.
Arguments:
- rho: float32 [256, 2, 256, 256], P(('groups', 'tier')), parts along dimension 0, may hold values from -6 to 6
- hamiltonian: float32 [256, 256], replicated, may hold values from -0.375 to 0.375
- couplings: float32 [4, 256, 256], replicated, may hold values from -0.375 to 0.375
- bath_coef: float32 [8, 2], P('groups'), parts along dimension 0, may hold values from 0.3 to 1.5
- damping: float32 [256], P(('groups', 'tier')), parts along dimension 0, may hold values from 0.2 to 3
- match_edges: int32 [16, 4, 1, 5], P('tier'), may hold values from 0 to 7, as said below
- left_rows: int32 [16, 6, 5], replicated, may hold values from 0 to 127, as said below
- left_count: int32 [16], replicated, may hold values from 1 to 6, as said below
Outputs:
- rho_next: float32 [256, 2, 256, 256], P(('groups', 'tier')), parts along dimension 0
The draws below stay inside these ranges and needn't reach their ends.
There are 2 independent parts, one for each index of `groups`. The reference program is written for one: setup_inputs(seed, part) draws one part's arguments, and reference() takes and returns one part's arrays. A program takes and returns all parts, laid end to end along the dimension named above; an argument that names none is the same for every part. Nothing has to cross between parts.
Inputs may be any that keep to these rules, and one draw needn't show every extreme that they name: match_edges[b, c, j] = (target slot, partner slot, mode, lower flag 0 or 1, occupation 1 to 3); the row (b XOR 2^c, c, j) describes the same edge from the partner's side: its target slot is this row's partner slot and the reverse, same mode and occupation, opposite lower flag. left_rows[b, j] = (target slot, source matrix index, mode, lower flag 0 or 1, occupation 1 to 3); the source's block lies at cyclic block distance 1 to 4 from b, and the rows of one block name distinct source blocks. Only the first left_count[b] rows of block b are live; some block has exactly 6.
All inputs are finite; a program needn't handle non-finite values.
Results may differ from the reference program's by a relative error of at most 0.00005.
Values sent between devices are 32-bit elements; how exact they have to be, the bound alone decides.
No kernel may reach another device: no remote copies, remote signals or barrier semaphores. Data moves between devices by JAX's collectives and lax.ppermute only.
A program may use at most 128 MiB of HBM per device.

```python
import math
import jax
import jax.numpy as jnp
from jax import lax

ORDER = 256
KMODES = 4
COLOURS = 4
PAIRS = 1
LEFT_CAP = 6
REACH = 4
MAT_DEV = 8
MATRICES = 128
N_TIER = 16


def match_tables(key):
    subkeys = jax.random.split(key, 4)
    blocks = jnp.arange(N_TIER, dtype=jnp.int32)
    slot_draw = jax.random.randint(subkeys[0], (COLOURS, N_TIER, PAIRS), 0, MAT_DEV)
    flag_draw = jax.random.randint(subkeys[1], (COLOURS, N_TIER, PAIRS), 0, 2)
    mode_draw = jax.random.randint(subkeys[2], (COLOURS, N_TIER, PAIRS), 0, KMODES)
    occ_draw = jax.random.randint(subkeys[3], (COLOURS, N_TIER, PAIRS), 1, 4)
    colour_rows = []
    for colour in range(COLOURS):
        stride = 2 ** colour
        upper_half = blocks // stride % 2
        partner = blocks + stride - 2 * stride * upper_half
        lowest = jnp.minimum(blocks, partner)
        own_slot = slot_draw[colour]
        their_slot = slot_draw[colour][partner]
        base_flag = flag_draw[colour][lowest]
        lower_flag = jnp.where(upper_half[:, None] == 0, base_flag, 1 - base_flag)
        mode_ids = mode_draw[colour][lowest]
        occupied = occ_draw[colour][lowest]
        colour_rows.append(jnp.stack([own_slot, their_slot, mode_ids, lower_flag, occupied], axis=-1))
    return jnp.stack(colour_rows, axis=1).astype(jnp.int32)


def draw_match_edges(key, part):
    return match_tables(jax.random.fold_in(key, 11))


def left_tables(key):
    subkeys = jax.random.split(key, 8)
    blocks = jnp.arange(N_TIER, dtype=jnp.int32)
    orders = jax.vmap(lambda sub: jax.random.permutation(sub, 2 * REACH))(jax.random.split(subkeys[0], N_TIER))
    picked = orders[:, :LEFT_CAP].astype(jnp.int32)
    offsets = jnp.where(picked < REACH, picked - REACH, picked - REACH + 1)
    src_block = (blocks[:, None] + offsets) % N_TIER
    src_slot = jax.random.randint(subkeys[1], (N_TIER, LEFT_CAP), 0, MAT_DEV)
    target_slot = jax.random.randint(subkeys[2], (N_TIER, LEFT_CAP), 0, MAT_DEV)
    mode_ids = jax.random.randint(subkeys[3], (N_TIER, LEFT_CAP), 0, KMODES)
    lower_flag = jax.random.randint(subkeys[4], (N_TIER, LEFT_CAP), 0, 2)
    occupied = jax.random.randint(subkeys[5], (N_TIER, LEFT_CAP), 1, 4)
    rows = jnp.stack([target_slot, src_block * MAT_DEV + src_slot, mode_ids, lower_flag, occupied], axis=-1)
    counts = jax.random.randint(subkeys[6], (N_TIER,), 1, LEFT_CAP // 2 + 1)
    busiest = jax.random.randint(subkeys[7], (), 0, N_TIER)
    counts = jnp.where(blocks == busiest, LEFT_CAP, counts)
    return (rows.astype(jnp.int32), counts.astype(jnp.int32))


def draw_left_rows(key, part):
    return left_tables(jax.random.fold_in(key, 23))[0]


def draw_left_count(key, part):
    return left_tables(jax.random.fold_in(key, 23))[1]


def levels(key, shape, shards, least, top_value):
    level, own = 1.0, jax.random.fold_in(key, 6)
    for dim, parts in shards:
        draws = jnp.exp(jax.random.uniform(jax.random.fold_in(own, dim), (parts,), jnp.float32, least / len(shards), top_value / len(shards)))
        level = level * jnp.repeat(draws, shape[dim] // parts).reshape([-1 if axis == dim else 1 for axis in range(len(shape))])
    return level


def gaussian(key, extent, scale, limit, cuts=(), kind=jnp.bfloat16):
    factor_of = levels(key, extent, cuts, -0.22, 0.18) if cuts else 1.0
    drawn = jax.random.normal(key, extent, jnp.float32) * scale * factor_of
    return jnp.minimum(jnp.maximum(drawn, -limit), limit).astype(kind)


def setup_inputs(seed: int = 0, part: int = 0) -> dict:
    seeds = jax.random.split(jax.random.key(seed), 9)
    part_splits = jax.random.split(jax.random.fold_in(seeds[8], part), 9)
    rho = gaussian(part_splits[0], (MATRICES, 2, ORDER, ORDER), 1.0, 6.0, ((0, 16),), jnp.float32)
    hamiltonian = gaussian(seeds[1], (ORDER, ORDER), ORDER ** -0.5, 0.375, (), jnp.float32)
    couplings = gaussian(seeds[2], (KMODES, ORDER, ORDER), ORDER ** -0.5, 0.375, (), jnp.float32)
    bath_coef = jnp.clip(jax.random.uniform(part_splits[3], (KMODES, 2), jnp.float32, 0.3, 1.5), 0.3, 1.5)
    damping = jnp.clip(jnp.exp(math.log(3.0) - 2.7080502 * jax.random.uniform(part_splits[4], (MATRICES,), jnp.float32) ** levels(part_splits[4], (MATRICES,), ((0, 16),), -0.2, 0.2)), 0.2, 3.0)
    match_edges = draw_match_edges(jax.random.fold_in(seeds[8], 71), part)
    left_rows = draw_left_rows(jax.random.fold_in(seeds[8], 71), part)
    left_count = draw_left_count(jax.random.fold_in(seeds[8], 71), part)
    return dict(rho=rho, hamiltonian=hamiltonian, couplings=couplings, bath_coef=bath_coef, damping=damping, match_edges=match_edges, left_rows=left_rows, left_count=left_count)


step_size = 0.1

def commute_hamiltonian(density, hamiltonian):
    left_side = jnp.einsum('ab,nxbc->nxac', hamiltonian, density, precision=lax.Precision.HIGHEST)
    right_side = jnp.einsum('nxab,bc->nxac', density, hamiltonian, precision=lax.Precision.HIGHEST)
    difference = left_side - right_side
    return jnp.stack([difference[:, 1], -difference[:, 0]], axis=1)

def edge_terms(sources, mode_ids, lower_flags, occupied, couplings, bath_coef):
    chosen = jnp.take(couplings, mode_ids, axis=0)
    left_prod = jnp.einsum('rab,rxbc->rxac', chosen, sources, precision=lax.Precision.HIGHEST)
    right_prod = jnp.einsum('rxab,rbc->rxac', sources, chosen, precision=lax.Precision.HIGHEST)
    is_lower = lower_flags == 1
    real_coef = jnp.where(is_lower, jnp.ones_like(bath_coef[:, 0])[0], jnp.take(bath_coef[:, 0], mode_ids))
    imag_coef = jnp.where(is_lower, jnp.zeros_like(bath_coef[:, 1])[0], jnp.take(bath_coef[:, 1], mode_ids))
    root_occ = jnp.sqrt(occupied.astype(jnp.float32))
    difference = left_prod - right_prod
    summed = left_prod + right_prod
    real_part = real_coef[:, None, None] * difference[:, 0] - imag_coef[:, None, None] * summed[:, 1]
    imag_part = real_coef[:, None, None] * difference[:, 1] + imag_coef[:, None, None] * summed[:, 0]
    return root_occ[:, None, None, None] * jnp.stack([imag_part, -real_part], axis=1)

def reference(rho, hamiltonian, couplings, bath_coef, damping, match_edges, left_rows, left_count):
    blocks = jnp.arange(N_TIER, dtype=jnp.int32)
    targets, anchors, mode_ids, lower_flags, occupied, weights = ([], [], [], [], [], [])
    for colour in range(COLOURS):
        stride = 2 ** colour
        upper_half = blocks // stride % 2
        partner = blocks + stride - 2 * stride * upper_half
        edge_table = match_edges[:, colour]
        targets.append((blocks[:, None] * MAT_DEV + edge_table[:, :, 0]).reshape(-1))
        anchors.append((partner[:, None] * MAT_DEV + edge_table[:, :, 1]).reshape(-1))
        mode_ids.append(edge_table[:, :, 2].reshape(-1))
        lower_flags.append(edge_table[:, :, 3].reshape(-1))
        occupied.append(edge_table[:, :, 4].reshape(-1))
        weights.append(jnp.ones((N_TIER * PAIRS,), jnp.float32))
    live_rows = jnp.arange(LEFT_CAP, dtype=jnp.int32)[None, :] < left_count[:, None]
    targets.append((blocks[:, None] * MAT_DEV + left_rows[:, :, 0]).reshape(-1))
    anchors.append(left_rows[:, :, 1].reshape(-1))
    mode_ids.append(left_rows[:, :, 2].reshape(-1))
    lower_flags.append(left_rows[:, :, 3].reshape(-1))
    occupied.append(left_rows[:, :, 4].reshape(-1))
    weights.append(live_rows.reshape(-1).astype(jnp.float32))
    targets = jnp.concatenate(targets).astype(jnp.int32)
    anchors = jnp.concatenate(anchors).astype(jnp.int32)
    mode_ids = jnp.concatenate(mode_ids).astype(jnp.int32)
    lower_flags = jnp.concatenate(lower_flags)
    occupied = jnp.concatenate(occupied)
    weights = jnp.concatenate(weights)

    def derivative(density):
        sources = jnp.take(density, anchors, axis=0)
        row_terms = edge_terms(sources, mode_ids, lower_flags, occupied, couplings, bath_coef)
        row_terms = row_terms * weights[:, None, None, None]
        coupled = jax.ops.segment_sum(row_terms, targets, num_segments=MATRICES)
        return commute_hamiltonian(density, hamiltonian) - damping[:, None, None, None] * density + coupled
    first_slope = derivative(rho)
    middle = rho + step_size * first_slope
    second_slope = derivative(middle)
    return rho + 0.5 * step_size * (first_slope + second_slope)
```

```python
import functools

import jax
import jax.numpy as jnp
from jax import lax
from jax.experimental import pallas as pl
from jax.experimental.pallas import tpu as pltpu
from jax.sharding import PartitionSpec as P

REACH = 4
STEP = 0.1
F32, BF16 = jnp.float32, jnp.bfloat16
SMEM = pl.BlockSpec(memory_space=pltpu.SMEM)
VMEM = pl.BlockSpec(memory_space=pltpu.VMEM)
ANY = pl.BlockSpec(memory_space=pl.ANY)


class Exchange:
    def __init__(self, kind, step, size, colour=None, listed=True):
        self.kind, self.step, self.size, self.colour, self.listed = kind, step, size, colour, listed

    def peer(self, index, outgoing):
        size, step = self.size, self.step
        if self.kind == "swap":
            return index ^ step
        if self.kind == "other":
            lower = (index & step) == 0
            if isinstance(index, int):
                return (index + (-step if lower else step)) % size
            return lax.rem(index + jnp.where(lower, size - step, step), size)
        move = step if outgoing else size - step
        if isinstance(index, int):
            return (index + move) % size
        return lax.rem(index + move, size)

    def permute(self, value):
        return lax.ppermute(value, "tier", [(i, self.peer(i, True)) for i in range(self.size)])


def exchanges(size, colours):
    near, far = [], []
    for distance in range(1, REACH + 1):
        colour = distance.bit_length() - 1
        if distance == 1 << colour and colour < colours:
            group = [
                Exchange("swap", distance, size, colour),
                Exchange("other", distance, size),
            ]
        else:
            group = [Exchange("shift", distance, size), Exchange("shift", size - distance, size)]
        (near if distance < REACH else far).extend(group)
    for colour in range(colours):
        if 1 << colour > REACH:
            far.append(Exchange("swap", 1 << colour, size, colour, listed=False))
    return near + far


def payload(exchange, pairs):
    return (pairs if exchange.colour is not None else 0) + (1 if exchange.listed else 0)


def split(value):
    high = value.astype(BF16)
    return high, (value - high.astype(F32)).astype(BF16)


def product(left, right):
    dot = functools.partial(jnp.dot, preferred_element_type=F32)
    return dot(left[0], right[0]) + (dot(left[0], right[1]) + dot(left[1], right[0]))


def outgoing_slots(exchange, me, mats, left_ref, count_ref, match_ref):
    slots = []
    if exchange.colour is not None:
        for j in range(match_ref.shape[2]):
            slots.append(match_ref[0, exchange.colour, j, 0])
    if exchange.listed:
        peer = exchange.peer(me, True)
        slot = jnp.int32(0)
        for j in range(left_ref.shape[1]):
            source = left_ref[peer, j, 1]
            hit = (j < count_ref[peer]) & (lax.div(source, mats) == me)
            slot = jnp.where(hit, lax.rem(source, mats), slot)
        slots.append(slot)
    return slots


def incoming_rows(exchange, me, mats, left_ref, count_ref, match_ref, left_root, match_root, bath_ref):
    rows = []

    def row(live, target, mode, flag, root):
        lower = flag == 1
        a = jnp.where(lower, jnp.float32(1), bath_ref[mode, 0])
        b = jnp.where(lower, jnp.float32(0), bath_ref[mode, 1])
        rows.append((live, target, mode, a * root, b * root))

    if exchange.colour is not None:
        c = exchange.colour
        for j in range(match_ref.shape[2]):
            row(None, match_ref[0, c, j, 0], match_ref[0, c, j, 2], match_ref[0, c, j, 3], match_root[c, j])
    if exchange.listed:
        peer = exchange.peer(me, False)
        found = [jnp.int32(0)] * 4 + [jnp.float32(0)]
        for j in range(left_ref.shape[1]):
            hit = (j < count_ref[me]) & (lax.div(left_ref[me, j, 1], mats) == peer)
            here = [1, left_ref[me, j, 0], left_ref[me, j, 2], left_ref[me, j, 3], left_root[me, j]]
            found = [jnp.where(hit, new, old) for new, old in zip(here, found)]
        row(found[0] == 1, found[1], found[2], found[3], found[4])
    return rows


def pack_kernel(plan, mats, me_ref, left_ref, count_ref, match_ref, source, *rest):
    sends, sems = rest[:-1], rest[-1]
    pack(plan, mats, me_ref, left_ref, count_ref, match_ref, source, sends, sems)


def pack(plan, mats, me_ref, left_ref, count_ref, match_ref, source, sends, sems):
    copies = []
    for exchange, send in zip(plan, sends):
        slots = outgoing_slots(exchange, me_ref[0], mats, left_ref, count_ref, match_ref)
        for place, slot in enumerate(slots):
            copies.append(pltpu.make_async_copy(source.at[slot], send.at[place], sems.at[len(copies)]))
            copies[-1].start()
    for copy in copies:
        copy.wait()


def commutator(density, hamiltonian):
    parts = []
    for part in (density[0], density[1]):
        halves = split(part)
        parts.append(product(hamiltonian, halves) - product(halves, hamiltonian))
    return parts[1], -parts[0]


def first_local_kernel(damping_ref, hamiltonian_ref, rho_ref, out_ref):
    decay = damping_ref[pl.program_id(0)]
    density = (rho_ref[0, 0], rho_ref[0, 1])
    turned = commutator(density, split(hamiltonian_ref[...]))
    for part in range(2):
        out_ref[0, part] = turned[part] - decay * density[part]


def second_local_kernel(damping_ref, hamiltonian_ref, first_ref, rho_ref, out_ref):
    decay = damping_ref[pl.program_id(0)]
    density = (first_ref[0, 0], first_ref[0, 1])
    turned = commutator(density, split(hamiltonian_ref[...]))
    for part in range(2):
        slope = turned[part] - decay * density[part]
        out_ref[0, part] = rho_ref[0, part] + STEP * density[part] + (0.5 * STEP * STEP) * slope


def local_call(kernel, damping, hamiltonian, *densities):
    mats, _, order, _ = densities[0].shape
    block = pl.BlockSpec((1, 2, order, order), lambda n: (n, 0, 0, 0))
    return pl.pallas_call(
        kernel,
        grid=(mats,),
        in_specs=[SMEM, pl.BlockSpec((order, order), lambda n: (0, 0))] + [block] * len(densities),
        out_specs=block,
        out_shape=jax.ShapeDtypeStruct(densities[0].shape, F32),
        compiler_params=pltpu.CompilerParams(vmem_limit_bytes=32 * 1024 * 1024),
        cost_estimate=pl.CostEstimate(
            flops=mats * 24 * order**3, bytes_accessed=mats * 16 * order**2 * (1 + len(densities)), transcendentals=0
        ),
    )(damping, hamiltonian, *densities)


def rows_kernel(plan, packs, scale, refs_in, *refs):
    me_ref, left_ref, count_ref, match_ref, left_root, match_root, bath_ref = refs[:7]
    couplings_ref = refs[7]
    arrivals = refs[8 : 8 + len(plan)]
    acc_in = refs[8 + len(plan)]
    rest = refs[9 + len(plan) :]
    acc_out, sends = rest[0], rest[1 : 1 + len(packs)]
    acc, landed, acc_sems, land_sems, send_sems = rest[1 + len(packs) :]
    mats = acc.shape[0]
    loads = [pltpu.make_async_copy(acc_in.at[n], acc.at[n], acc_sems.at[n]) for n in range(mats)]
    rows, lands = [], []
    for exchange, arrival in zip(plan, arrivals):
        found = incoming_rows(
            exchange, me_ref[0], mats, left_ref, count_ref, match_ref, left_root, match_root, bath_ref
        )
        for place, row in enumerate(found):
            at = len(rows)
            lands.append(pltpu.make_async_copy(arrival.at[place], landed.at[at], land_sems.at[at]))
            rows.append(row)
    for land in lands:
        land.start()
    for load in loads:
        load.start()
    for load in loads:
        load.wait()
    for at, (live, target, mode, a, b) in enumerate(rows):
        lands[at].wait()

        def add(at=at, target=target, mode=mode, a=a, b=b):
            coupling = split(couplings_ref[mode])
            real, imag = split(landed[at, 0]), split(landed[at, 1])
            left_re, right_re = product(coupling, real), product(real, coupling)
            left_im, right_im = product(coupling, imag), product(imag, coupling)
            edge_re = a * (left_re - right_re) - b * (left_im + right_im)
            edge_im = a * (left_im - right_im) + b * (left_re + right_re)
            acc[target, 0] += scale * edge_im
            acc[target, 1] -= scale * edge_re

        if live is None:
            add()
        else:
            pl.when(live)(add)
    stores = [pltpu.make_async_copy(acc.at[n], acc_out.at[n], acc_sems.at[n]) for n in range(mats)]
    for store in stores:
        store.start()
    if packs:
        pack(packs, mats, me_ref, left_ref, count_ref, match_ref, acc, sends, send_sems)
    for store in stores:
        store.wait()


def rows_call(plan, packs, pairs, scale, tables, couplings, arrivals, acc):
    mats, _, order, _ = acc.shape
    count = sum(payload(e, pairs) for e in plan)
    sent = sum(payload(e, pairs) for e in packs)
    shapes = [jax.ShapeDtypeStruct(acc.shape, F32)]
    shapes += [jax.ShapeDtypeStruct((payload(e, pairs), 2, order, order), F32) for e in packs]
    return pl.pallas_call(
        functools.partial(rows_kernel, plan, packs, scale, None),
        in_specs=[SMEM] * 7 + [VMEM] + [ANY] * (len(plan) + 1),
        out_specs=[ANY] * len(shapes),
        out_shape=shapes,
        input_output_aliases={8 + len(plan): 0},
        scratch_shapes=[
            pltpu.VMEM((mats, 2, order, order), F32),
            pltpu.VMEM((count, 2, order, order), F32),
            pltpu.SemaphoreType.DMA((mats,)),
            pltpu.SemaphoreType.DMA((count,)),
            pltpu.SemaphoreType.DMA((max(sent, 1),)),
        ],
        compiler_params=pltpu.CompilerParams(vmem_limit_bytes=32 * 1024 * 1024),
        cost_estimate=pl.CostEstimate(
            flops=count * 24 * order**3, bytes_accessed=(count + 2 * mats + sent) * 8 * order**2, transcendentals=0
        ),
    )(*tables, couplings, *arrivals, acc)


def pack_call(plan, pairs, tables, source):
    mats, _, order, _ = source.shape
    sent = sum(payload(e, pairs) for e in plan)
    return pl.pallas_call(
        functools.partial(pack_kernel, plan, mats),
        in_specs=[SMEM] * 4 + [ANY],
        out_specs=[ANY] * len(plan),
        out_shape=[jax.ShapeDtypeStruct((payload(e, pairs), 2, order, order), F32) for e in plan],
        scratch_shapes=[pltpu.SemaphoreType.DMA((sent,))],
        cost_estimate=pl.CostEstimate(flops=0, bytes_accessed=sent * 16 * order**2, transcendentals=0),
    )(*tables[:4], source)


def body(rho, hamiltonian, couplings, bath_coef, damping, match_edges, left_rows, left_count):
    colours, pairs = match_edges.shape[1:3]
    plan = exchanges(lax.axis_size("tier"), colours)
    me = lax.axis_index("tier").astype(jnp.int32)[None]
    left_root = jnp.sqrt(left_rows[:, :, 4].astype(F32))
    match_root = jnp.sqrt(match_edges[0, :, :, 4].astype(F32))
    tables = (me, left_rows, left_count, match_edges, left_root, match_root, bath_coef)

    cuts = [0]
    for distance in (2, REACH - 1):
        cuts.append(max(i + 1 for i, e in enumerate(plan) if e.step in (distance, e.size - distance)))
    cuts.append(len(plan))
    groups = [slice(a, b) for a, b in zip(cuts, cuts[1:]) if a < b]

    def gather(sends, acc, scale, packs):
        arrived = [e.permute(s) for e, s in zip(plan, sends)]
        for group in groups:
            last = group is groups[-1]
            got = rows_call(
                plan[group], packs if last else [], pairs, scale, tables, couplings, arrived[group], acc
            )
            acc = got[0]
        return acc, got[1:]

    sends = pack_call(plan, pairs, tables, rho)
    first, sends = gather(sends, local_call(first_local_kernel, damping, hamiltonian, rho), 1.0, plan)
    base = local_call(second_local_kernel, damping, hamiltonian, first, rho)
    return gather(sends, base, 0.5 * STEP * STEP, [])[0]


def solution(mesh):
    placed = (
        P(("groups", "tier"), None, None, None),
        P(),
        P(),
        P("groups", None),
        P(("groups", "tier")),
        P("tier", None, None, None),
        P(),
        P(),
    )
    return jax.shard_map(
        body,
        mesh=mesh,
        in_specs=placed,
        out_specs=P(("groups", "tier"), None, None, None),
        check_vma=False,
    )
```

```python
import functools

import jax
import jax.numpy as jnp
from jax import lax
from jax.experimental import pallas as pl
from jax.experimental.pallas import tpu as pltpu
from jax.sharding import PartitionSpec as P

REACH = 4
STEP = 0.1
F32, BF16 = jnp.float32, jnp.bfloat16
SMEM = pl.BlockSpec(memory_space=pltpu.SMEM)
VMEM = pl.BlockSpec(memory_space=pltpu.VMEM)
ANY = pl.BlockSpec(memory_space=pl.ANY)


class Exchange:
    def __init__(self, kind, step, size, colour=None, listed=True):
        self.kind, self.step, self.size, self.colour, self.listed = kind, step, size, colour, listed

    def peer(self, index, outgoing):
        size, step = self.size, self.step
        if self.kind == "swap":
            return index ^ step
        if self.kind == "other":
            lower = (index & step) == 0
            if isinstance(index, int):
                return (index + (-step if lower else step)) % size
            return lax.rem(index + jnp.where(lower, size - step, step), size)
        move = step if outgoing else size - step
        if isinstance(index, int):
            return (index + move) % size
        return lax.rem(index + move, size)

    def permute(self, value):
        return lax.ppermute(value, "tier", [(i, self.peer(i, True)) for i in range(self.size)])


def exchanges(size, colours):
    near, far = [], []
    for distance in range(1, REACH + 1):
        colour = distance.bit_length() - 1
        if distance == 1 << colour and colour < colours:
            group = [
                Exchange("swap", distance, size, colour),
                Exchange("other", distance, size),
            ]
        else:
            group = [Exchange("shift", distance, size), Exchange("shift", size - distance, size)]
        (near if distance < REACH else far).extend(group)
    for colour in range(colours):
        if 1 << colour > REACH:
            far.append(Exchange("swap", 1 << colour, size, colour, listed=False))
    return near + far


def payload(exchange, pairs):
    return (pairs if exchange.colour is not None else 0) + (1 if exchange.listed else 0)


def split(value):
    high = value.astype(BF16)
    return high, (value - high.astype(F32)).astype(BF16)


def product(left, right):
    dot = functools.partial(jnp.dot, preferred_element_type=F32)
    return dot(left[0], right[0]) + (dot(left[0], right[1]) + dot(left[1], right[0]))


def outgoing_slots(exchange, me, mats, left_ref, count_ref, match_ref):
    slots = []
    if exchange.colour is not None:
        for j in range(match_ref.shape[2]):
            slots.append(match_ref[0, exchange.colour, j, 0])
    if exchange.listed:
        peer = exchange.peer(me, True)
        slot = jnp.int32(0)
        for j in range(left_ref.shape[1]):
            source = left_ref[peer, j, 1]
            hit = (j < count_ref[peer]) & (lax.div(source, mats) == me)
            slot = jnp.where(hit, lax.rem(source, mats), slot)
        slots.append(slot)
    return slots


def incoming_rows(exchange, me, mats, left_ref, count_ref, match_ref, left_root, match_root, bath_ref):
    rows = []

    def row(live, target, mode, flag, root):
        lower = flag == 1
        a = jnp.where(lower, jnp.float32(1), bath_ref[mode, 0])
        b = jnp.where(lower, jnp.float32(0), bath_ref[mode, 1])
        rows.append((live, target, mode, a * root, b * root))

    if exchange.colour is not None:
        c = exchange.colour
        for j in range(match_ref.shape[2]):
            row(None, match_ref[0, c, j, 0], match_ref[0, c, j, 2], match_ref[0, c, j, 3], match_root[c, j])
    if exchange.listed:
        peer = exchange.peer(me, False)
        found = [jnp.int32(0)] * 4 + [jnp.float32(0)]
        for j in range(left_ref.shape[1]):
            hit = (j < count_ref[me]) & (lax.div(left_ref[me, j, 1], mats) == peer)
            here = [1, left_ref[me, j, 0], left_ref[me, j, 2], left_ref[me, j, 3], left_root[me, j]]
            found = [jnp.where(hit, new, old) for new, old in zip(here, found)]
        row(found[0] == 1, found[1], found[2], found[3], found[4])
    return rows


def pack_kernel(plan, mats, me_ref, left_ref, count_ref, match_ref, source, *rest):
    sends, (held, load_sems, sems) = rest[:-3], rest[-3:]
    loads = [pltpu.make_async_copy(source.at[n], held.at[n], load_sems.at[n]) for n in range(mats)]
    for load in loads:
        load.start()
    for load in loads:
        load.wait()
    pack(plan, mats, me_ref, left_ref, count_ref, match_ref, held, sends, sems)


def pack(plan, mats, me_ref, left_ref, count_ref, match_ref, source, sends, sems):
    copies = []
    for exchange, send in zip(plan, sends):
        slots = outgoing_slots(exchange, me_ref[0], mats, left_ref, count_ref, match_ref)
        for place, slot in enumerate(slots):
            copies.append(pltpu.make_async_copy(source.at[slot], send.at[place], sems.at[len(copies)]))
            copies[-1].start()
    for copy in copies:
        copy.wait()


def commutator(density, hamiltonian):
    parts = []
    for part in (density[0], density[1]):
        halves = split(part)
        parts.append(product(hamiltonian, halves) - product(halves, hamiltonian))
    return parts[1], -parts[0]


def first_local_kernel(damping_ref, hamiltonian_ref, rho_ref, out_ref):
    decay = damping_ref[pl.program_id(0)]
    density = (rho_ref[0, 0], rho_ref[0, 1])
    turned = commutator(density, split(hamiltonian_ref[...]))
    for part in range(2):
        out_ref[0, part] = turned[part] - decay * density[part]


def second_local_kernel(damping_ref, hamiltonian_ref, first_ref, rho_ref, out_ref):
    decay = damping_ref[pl.program_id(0)]
    density = (first_ref[0, 0], first_ref[0, 1])
    turned = commutator(density, split(hamiltonian_ref[...]))
    for part in range(2):
        slope = turned[part] - decay * density[part]
        out_ref[0, part] = rho_ref[0, part] + STEP * density[part] + (0.5 * STEP * STEP) * slope


def local_call(kernel, damping, hamiltonian, *densities):
    mats, _, order, _ = densities[0].shape
    block = pl.BlockSpec((1, 2, order, order), lambda n: (n, 0, 0, 0))
    return pl.pallas_call(
        kernel,
        grid=(mats,),
        in_specs=[SMEM, pl.BlockSpec((order, order), lambda n: (0, 0))] + [block] * len(densities),
        out_specs=block,
        out_shape=jax.ShapeDtypeStruct(densities[0].shape, F32),
        compiler_params=pltpu.CompilerParams(vmem_limit_bytes=32 * 1024 * 1024),
        cost_estimate=pl.CostEstimate(
            flops=mats * 24 * order**3, bytes_accessed=mats * 16 * order**2 * (1 + len(densities)), transcendentals=0
        ),
    )(damping, hamiltonian, *densities)


def rows_kernel(plan, packs, scale, refs_in, *refs):
    me_ref, left_ref, count_ref, match_ref, left_root, match_root, bath_ref = refs[:7]
    couplings_ref = refs[7]
    arrivals = refs[8 : 8 + len(plan)]
    acc_in = refs[8 + len(plan)]
    rest = refs[9 + len(plan) :]
    acc_out, sends = rest[0], rest[1 : 1 + len(packs)]
    acc, landed, acc_sems, land_sems, send_sems = rest[1 + len(packs) :]
    mats = acc.shape[0]
    loads = [pltpu.make_async_copy(acc_in.at[n], acc.at[n], acc_sems.at[n]) for n in range(mats)]
    rows, lands = [], []
    for exchange, arrival in zip(plan, arrivals):
        found = incoming_rows(
            exchange, me_ref[0], mats, left_ref, count_ref, match_ref, left_root, match_root, bath_ref
        )
        for place, row in enumerate(found):
            at = len(rows)
            lands.append(pltpu.make_async_copy(arrival.at[place], landed.at[at], land_sems.at[at]))
            rows.append(row)
    for land in lands:
        land.start()
    for load in loads:
        load.start()
    for load in loads:
        load.wait()
    for at, (live, target, mode, a, b) in enumerate(rows):
        lands[at].wait()

        def add(at=at, target=target, mode=mode, a=a, b=b):
            coupling = split(couplings_ref[mode])
            real, imag = split(landed[at, 0]), split(landed[at, 1])
            left_re, right_re = product(coupling, real), product(real, coupling)
            left_im, right_im = product(coupling, imag), product(imag, coupling)
            edge_re = a * (left_re - right_re) - b * (left_im + right_im)
            edge_im = a * (left_im - right_im) + b * (left_re + right_re)
            acc[target, 0] += scale * edge_im
            acc[target, 1] -= scale * edge_re

        if live is None:
            add()
        else:
            pl.when(live)(add)
    stores = [pltpu.make_async_copy(acc.at[n], acc_out.at[n], acc_sems.at[n]) for n in range(mats)]
    for store in stores:
        store.start()
    if packs:
        pack(packs, mats, me_ref, left_ref, count_ref, match_ref, acc, sends, send_sems)
    for store in stores:
        store.wait()


def rows_call(plan, packs, pairs, scale, tables, couplings, arrivals, acc):
    mats, _, order, _ = acc.shape
    count = sum(payload(e, pairs) for e in plan)
    sent = sum(payload(e, pairs) for e in packs)
    shapes = [jax.ShapeDtypeStruct(acc.shape, F32)]
    shapes += [jax.ShapeDtypeStruct((payload(e, pairs), 2, order, order), F32) for e in packs]
    return pl.pallas_call(
        functools.partial(rows_kernel, plan, packs, scale, None),
        in_specs=[SMEM] * 7 + [VMEM] + [ANY] * (len(plan) + 1),
        out_specs=[ANY] * len(shapes),
        out_shape=shapes,
        input_output_aliases={8 + len(plan): 0},
        scratch_shapes=[
            pltpu.VMEM((mats, 2, order, order), F32),
            pltpu.VMEM((count, 2, order, order), F32),
            pltpu.SemaphoreType.DMA((mats,)),
            pltpu.SemaphoreType.DMA((count,)),
            pltpu.SemaphoreType.DMA((max(sent, 1),)),
        ],
        compiler_params=pltpu.CompilerParams(vmem_limit_bytes=32 * 1024 * 1024),
        cost_estimate=pl.CostEstimate(
            flops=count * 24 * order**3, bytes_accessed=(count + 2 * mats + sent) * 8 * order**2, transcendentals=0
        ),
    )(*tables, couplings, *arrivals, acc)


def pack_call(plan, pairs, tables, source):
    mats, _, order, _ = source.shape
    sent = sum(payload(e, pairs) for e in plan)
    return pl.pallas_call(
        functools.partial(pack_kernel, plan, mats),
        in_specs=[SMEM] * 4 + [ANY],
        out_specs=[ANY] * len(plan),
        out_shape=[jax.ShapeDtypeStruct((payload(e, pairs), 2, order, order), F32) for e in plan],
        scratch_shapes=[
            pltpu.VMEM(source.shape, F32),
            pltpu.SemaphoreType.DMA((mats,)),
            pltpu.SemaphoreType.DMA((sent,)),
        ],
        compiler_params=pltpu.CompilerParams(vmem_limit_bytes=16 * 1024 * 1024),
        cost_estimate=pl.CostEstimate(flops=0, bytes_accessed=sent * 16 * order**2, transcendentals=0),
    )(*tables[:4], source)


def body(rho, hamiltonian, couplings, bath_coef, damping, match_edges, left_rows, left_count):
    colours, pairs = match_edges.shape[1:3]
    plan = exchanges(lax.axis_size("tier"), colours)
    me = lax.axis_index("tier").astype(jnp.int32)[None]
    left_root = jnp.sqrt(left_rows[:, :, 4].astype(F32))
    match_root = jnp.sqrt(match_edges[0, :, :, 4].astype(F32))
    tables = (me, left_rows, left_count, match_edges, left_root, match_root, bath_coef)

    cuts = [0]
    for distance in (2, REACH - 1):
        cuts.append(max(i + 1 for i, e in enumerate(plan) if e.step in (distance, e.size - distance)))
    cuts.append(len(plan))
    groups = [slice(a, b) for a, b in zip(cuts, cuts[1:]) if a < b]

    def gather(sends, acc, scale, packs):
        arrived = [e.permute(s) for e, s in zip(plan, sends)]
        for group in groups:
            last = group is groups[-1]
            got = rows_call(
                plan[group], packs if last else [], pairs, scale, tables, couplings, arrived[group], acc
            )
            acc = got[0]
        return acc, got[1:]

    sends = pack_call(plan, pairs, tables, rho)
    first, sends = gather(sends, local_call(first_local_kernel, damping, hamiltonian, rho), 1.0, plan)
    base = local_call(second_local_kernel, damping, hamiltonian, first, rho)
    return gather(sends, base, 0.5 * STEP * STEP, [])[0]


def solution(mesh):
    placed = (
        P(("groups", "tier"), None, None, None),
        P(),
        P(),
        P("groups", None),
        P(("groups", "tier")),
        P("tier", None, None, None),
        P(),
        P(),
    )
    return jax.shard_map(
        body,
        mesh=mesh,
        in_specs=placed,
        out_specs=P(("groups", "tier"), None, None, None),
        check_vma=False,
    )
```

```python
import functools

import jax
import jax.numpy as jnp
from jax import lax
from jax.experimental import pallas as pl
from jax.experimental.pallas import tpu as pltpu
from jax.sharding import PartitionSpec as P

REACH = 4
STEP = 0.1
F32, BF16 = jnp.float32, jnp.bfloat16
SMEM = pl.BlockSpec(memory_space=pltpu.SMEM)
VMEM = pl.BlockSpec(memory_space=pltpu.VMEM)
HBM = pl.BlockSpec(memory_space=pltpu.HBM)
GRANT = 56 * 1024 * 1024


class Exchange:
    def __init__(self, kind, step, size, colour=None, listed=True):
        self.kind, self.step, self.size, self.colour, self.listed = kind, step, size, colour, listed

    def peer(self, index, outgoing):
        size, step = self.size, self.step
        if self.kind == "swap":
            return index ^ step
        if self.kind == "other":
            lower = (index & step) == 0
            if isinstance(index, int):
                return (index + (-step if lower else step)) % size
            return lax.rem(index + jnp.where(lower, size - step, step), size)
        move = step if outgoing else size - step
        if isinstance(index, int):
            return (index + move) % size
        return lax.rem(index + move, size)

    def permute(self, value):
        return lax.ppermute(value, "tier", [(i, self.peer(i, True)) for i in range(self.size)])


def exchanges(size, colours):
    swaps, others, shifts, far = [], [], [], []
    for colour in range(colours):
        if 1 << colour > REACH:
            far.append(Exchange("swap", 1 << colour, size, colour, listed=False))
    for distance in range(1, REACH + 1):
        colour = distance.bit_length() - 1
        if distance != 1 << colour or colour >= colours:
            shifts += [Exchange("shift", distance, size), Exchange("shift", size - distance, size)]
        elif distance < REACH:
            swaps.append(Exchange("swap", distance, size, colour))
            others.insert(0, Exchange("other", distance, size))
        else:
            far += [Exchange("swap", distance, size, colour), Exchange("other", distance, size)]
    return swaps, shifts + others, far


def payload(exchange, pairs):
    return (pairs if exchange.colour is not None else 0) + (1 if exchange.listed else 0)


def when(condition, action):
    if condition is None:
        action()
    else:
        pl.when(condition)(action)


def split(value):
    high = value.astype(BF16)
    return high, (value - high.astype(F32)).astype(BF16)


def product(left, right):
    dot = functools.partial(jnp.dot, preferred_element_type=F32)
    return dot(left[0], right[0]) + (dot(left[0], right[1]) + dot(left[1], right[0]))


def outgoing_slots(exchange, me, mats, left_ref, count_ref, match_ref):
    slots = []
    if exchange.colour is not None:
        for j in range(match_ref.shape[2]):
            slots.append(match_ref[0, exchange.colour, j, 0])
    if exchange.listed:
        peer = exchange.peer(me, True)
        slot = jnp.int32(0)
        for j in range(left_ref.shape[1]):
            source = left_ref[1, j, peer]
            hit = (j < count_ref[peer]) & (lax.div(source, mats) == me)
            slot = jnp.where(hit, lax.rem(source, mats), slot)
        slots.append(slot)
    return slots


def incoming_rows(exchange, me, mats, left_ref, count_ref, match_ref, left_root, match_root, bath_ref):
    rows = []

    def row(live, target, mode, flag, root):
        lower = flag == 1
        a = jnp.where(lower, jnp.float32(1), bath_ref[0, mode])
        b = jnp.where(lower, jnp.float32(0), bath_ref[1, mode])
        rows.append((live, target, mode, a * root, b * root))

    if exchange.colour is not None:
        c = exchange.colour
        for j in range(match_ref.shape[2]):
            row(None, match_ref[0, c, j, 0], match_ref[0, c, j, 2], match_ref[0, c, j, 3], match_root[c, j])
    if exchange.listed:
        peer = exchange.peer(me, False)
        found = [jnp.int32(0)] * 4 + [jnp.float32(0)]
        for j in range(left_ref.shape[1]):
            hit = (j < count_ref[me]) & (lax.div(left_ref[1, j, me], mats) == peer)
            here = [1, left_ref[0, j, me], left_ref[2, j, me], left_ref[3, j, me], left_root[j, me]]
            found = [jnp.where(hit, new, old) for new, old in zip(here, found)]
        row(found[0] == 1, found[1], found[2], found[3], found[4])
    return rows


def pack_kernel(plan, mats, me_ref, left_ref, count_ref, match_ref, source, *rest):
    sends, (held, load_sems, sems) = rest[:-3], rest[-3:]
    loads = [pltpu.make_async_copy(source.at[n], held.at[n], load_sems.at[n]) for n in range(mats)]
    for load in loads:
        load.start()
    for load in loads:
        load.wait()
    pack(plan, mats, me_ref, left_ref, count_ref, match_ref, held, sends, sems)


def pack(plan, mats, me_ref, left_ref, count_ref, match_ref, source, sends, sems):
    copies = []
    for exchange, send in zip(plan, sends):
        slots = outgoing_slots(exchange, me_ref[0], mats, left_ref, count_ref, match_ref)
        for place, slot in enumerate(slots):
            copies.append(pltpu.make_async_copy(source.at[slot], send.at[place], sems.at[len(copies)]))
            copies[-1].start()
    for copy in copies:
        copy.wait()


def commutator(density, hamiltonian):
    parts = []
    for part in (density[0], density[1]):
        halves = split(part)
        parts.append(product(hamiltonian, halves) - product(halves, hamiltonian))
    return parts[1], -parts[0]


def local_kernel(packs, second, me_ref, left_ref, count_ref, match_ref, damping_ref, hamiltonian_ref, *refs):
    density_ref, refs = refs[0], refs[1:]
    if second:
        rho_ref, refs = refs[0], refs[1:]
    out_ref, sends, sems = refs[0], refs[1:-1], refs[-1]
    here, mats = pl.program_id(0), pl.num_programs(0)
    copies = []
    for exchange, send in zip(packs, sends):
        slots = outgoing_slots(exchange, me_ref[0], mats, left_ref, count_ref, match_ref)
        for place, slot in enumerate(slots):
            copy = pltpu.make_async_copy(density_ref.at[0], send.at[place], sems.at[len(copies)])
            copies.append((slot == here, copy))
    for asked, copy in copies:
        pl.when(asked)(copy.start)
    decay = damping_ref[here]
    density = (density_ref[0, 0], density_ref[0, 1])
    turned = commutator(density, split(hamiltonian_ref[...]))
    for part in range(2):
        slope = turned[part] - decay * density[part]
        if second:
            slope = rho_ref[0, part] + STEP * density[part] + (0.5 * STEP * STEP) * slope
        out_ref[0, part] = slope
    for asked, copy in copies:
        pl.when(asked)(copy.wait)


def local_call(packs, pairs, tables, damping, hamiltonian, *densities):
    mats, _, order, _ = densities[0].shape
    sent = sum(payload(e, pairs) for e in packs)
    block = pl.BlockSpec((1, 2, order, order), lambda n: (n, 0, 0, 0))
    return pl.pallas_call(
        functools.partial(local_kernel, packs, len(densities) == 2),
        grid=(mats,),
        in_specs=[SMEM] * 5 + [pl.BlockSpec((order, order), lambda n: (0, 0))] + [block] * len(densities),
        out_specs=[block] + [HBM] * len(packs),
        out_shape=[jax.ShapeDtypeStruct(densities[0].shape, F32)]
        + [jax.ShapeDtypeStruct((payload(e, pairs), 2, order, order), F32) for e in packs],
        scratch_shapes=[pltpu.SemaphoreType.DMA((sent,))],
        compiler_params=pltpu.CompilerParams(vmem_limit_bytes=GRANT),
        cost_estimate=pl.CostEstimate(
            flops=mats * 24 * order**3,
            bytes_accessed=(mats * (1 + len(densities)) + sent) * 8 * order**2,
            transcendentals=0,
        ),
    )(*tables[:4], damping, hamiltonian, *densities)


def rows_kernel(plan, packs, scale, *refs):
    me_ref, left_ref, count_ref, match_ref, left_root, match_root, bath_ref = refs[:7]
    couplings_ref = refs[7]
    arrivals = refs[8 : 8 + len(plan)]
    acc_in = refs[8 + len(plan)]
    rest = refs[9 + len(plan) :]
    acc_out, sends = rest[0], rest[1 : 1 + len(packs)]
    acc, landed, acc_sems, land_sems, send_sems = rest[1 + len(packs) :]
    mats = acc.shape[0]
    loads = [pltpu.make_async_copy(acc_in.at[n], acc.at[n], acc_sems.at[n]) for n in range(mats)]
    rows, lands = [], []
    for exchange, arrival in zip(plan, arrivals):
        found = incoming_rows(
            exchange, me_ref[0], mats, left_ref, count_ref, match_ref, left_root, match_root, bath_ref
        )
        for place, row in enumerate(found):
            at = len(rows)
            lands.append(pltpu.make_async_copy(arrival.at[place], landed.at[at], land_sems.at[at]))
            rows.append(row)
    for (live, *_), land in zip(rows, lands):
        when(live, land.start)
    touched = []
    for n in range(mats):
        hits = [row[1] == n if row[0] is None else row[0] & (row[1] == n) for row in rows]
        touched.append(None if packs else functools.reduce(jnp.logical_or, hits))
        when(touched[n], loads[n].start)
    for n in range(mats):
        when(touched[n], loads[n].wait)
    for at, (live, target, mode, a, b) in enumerate(rows):
        def add(at=at, target=target, mode=mode, a=a, b=b):
            lands[at].wait()
            coupling = split(couplings_ref[mode])
            real, imag = split(landed[at, 0]), split(landed[at, 1])
            left_re, right_re = product(coupling, real), product(real, coupling)
            left_im, right_im = product(coupling, imag), product(imag, coupling)
            edge_re = a * (left_re - right_re) - b * (left_im + right_im)
            edge_im = a * (left_im - right_im) + b * (left_re + right_re)
            acc[target, 0] += scale * edge_im
            acc[target, 1] -= scale * edge_re

        when(live, add)
    stores = [pltpu.make_async_copy(acc.at[n], acc_out.at[n], acc_sems.at[n]) for n in range(mats)]
    for n in range(mats):
        when(touched[n], stores[n].start)
    if packs:
        pack(packs, mats, me_ref, left_ref, count_ref, match_ref, acc, sends, send_sems)
    for n in range(mats):
        when(touched[n], stores[n].wait)


def rows_call(plan, packs, pairs, scale, tables, couplings, arrivals, acc):
    mats, _, order, _ = acc.shape
    count = sum(payload(e, pairs) for e in plan)
    sent = sum(payload(e, pairs) for e in packs)
    shapes = [jax.ShapeDtypeStruct(acc.shape, F32)]
    shapes += [jax.ShapeDtypeStruct((payload(e, pairs), 2, order, order), F32) for e in packs]
    return pl.pallas_call(
        functools.partial(rows_kernel, plan, packs, scale),
        in_specs=[SMEM] * 7 + [VMEM] + [HBM] * (len(plan) + 1),
        out_specs=[HBM] * len(shapes),
        out_shape=shapes,
        input_output_aliases={8 + len(plan): 0},
        scratch_shapes=[
            pltpu.VMEM((mats, 2, order, order), F32),
            pltpu.VMEM((count, 2, order, order), F32),
            pltpu.SemaphoreType.DMA((mats,)),
            pltpu.SemaphoreType.DMA((count,)),
            pltpu.SemaphoreType.DMA((max(sent, 1),)),
        ],
        compiler_params=pltpu.CompilerParams(vmem_limit_bytes=GRANT),
        cost_estimate=pl.CostEstimate(
            flops=count * 24 * order**3, bytes_accessed=(count + 2 * mats + sent) * 8 * order**2, transcendentals=0
        ),
    )(*tables, couplings, *arrivals, acc)


def pack_call(plan, pairs, tables, source):
    mats, _, order, _ = source.shape
    sent = sum(payload(e, pairs) for e in plan)
    return pl.pallas_call(
        functools.partial(pack_kernel, plan, mats),
        in_specs=[SMEM] * 4 + [HBM],
        out_specs=[HBM] * len(plan),
        out_shape=[jax.ShapeDtypeStruct((payload(e, pairs), 2, order, order), F32) for e in plan],
        scratch_shapes=[
            pltpu.VMEM(source.shape, F32),
            pltpu.SemaphoreType.DMA((mats,)),
            pltpu.SemaphoreType.DMA((sent,)),
        ],
        compiler_params=pltpu.CompilerParams(vmem_limit_bytes=GRANT),
        cost_estimate=pl.CostEstimate(flops=0, bytes_accessed=sent * 16 * order**2, transcendentals=0),
    )(*tables[:4], source)


def body(rho, hamiltonian, couplings, bath_coef, damping, match_edges, left_rows, left_count):
    colours, pairs = match_edges.shape[1:3]
    swaps, shifts, far = exchanges(lax.axis_size("tier"), colours)
    me = lax.axis_index("tier").astype(jnp.int32)[None]
    left_fields = jnp.transpose(left_rows, (2, 1, 0))
    left_root = jnp.sqrt(left_fields[4].astype(F32))
    match_root = jnp.sqrt(match_edges[0, :, :, 4].astype(F32))
    tables = (me, left_fields, left_count, match_edges, left_root, match_root, bath_coef.T)

    def gather(near_sends, far_sends, acc, scale, packs):
        sends = list(near_sends) + list(far_sends)
        arrived = [e.permute(s) for e, s in zip(swaps + shifts + far, sends)]
        for group in (swaps, shifts, far):
            got = rows_call(
                group, packs if group is far else [], pairs, scale, tables, couplings, arrived[: len(group)], acc
            )
            acc, arrived = got[0], arrived[len(group) :]
        return acc, got[1:]

    near = swaps + shifts
    sends = pack_call(near, pairs, tables, rho)
    base, *far_sends = local_call(far, pairs, tables, damping, hamiltonian, rho)
    first, sends = gather(sends, far_sends, base, 1.0, near)
    base, *far_sends = local_call(far, pairs, tables, damping, hamiltonian, first, rho)
    return gather(sends, far_sends, base, 0.5 * STEP * STEP, [])[0]


def solution(mesh):
    placed = (
        P(("groups", "tier"), None, None, None),
        P(),
        P(),
        P("groups", None),
        P(("groups", "tier")),
        P("tier", None, None, None),
        P(),
        P(),
    )
    return jax.shard_map(
        body,
        mesh=mesh,
        in_specs=placed,
        out_specs=P(("groups", "tier"), None, None, None),
        check_vma=False,
    )
```

```python
import functools

import jax
import jax.numpy as jnp
from jax import lax
from jax.experimental import pallas as pl
from jax.experimental.pallas import tpu as pltpu
from jax.sharding import PartitionSpec as P

REACH = 4
STEP = 0.1
F32, BF16 = jnp.float32, jnp.bfloat16
SMEM = pl.BlockSpec(memory_space=pltpu.SMEM)
HBM = pl.BlockSpec(memory_space=pltpu.HBM)
ANY = pl.BlockSpec(memory_space=pl.ANY)
GRANT = 48 * 1024 * 1024


class Exchange:
    def __init__(self, kind, step, size, colour=None, listed=True):
        self.kind, self.step, self.size, self.colour, self.listed = kind, step, size, colour, listed

    def peer(self, index, outgoing):
        size, step = self.size, self.step
        if self.kind == "swap":
            return index ^ step
        if self.kind == "other":
            lower = (index & step) == 0
            if isinstance(index, int):
                return (index + (-step if lower else step)) % size
            return lax.rem(index + jnp.where(lower, size - step, step), size)
        move = step if outgoing else size - step
        if isinstance(index, int):
            return (index + move) % size
        return lax.rem(index + move, size)

    def permute(self, value):
        return lax.ppermute(value, "tier", [(i, self.peer(i, True)) for i in range(self.size)])


def exchanges(size, colours):
    swaps, others, shifts, far = [], [], [], []
    for colour in range(colours):
        if 1 << colour > REACH:
            far.append(Exchange("swap", 1 << colour, size, colour, listed=False))
    for distance in range(1, REACH + 1):
        colour = distance.bit_length() - 1
        if distance != 1 << colour or colour >= colours:
            shifts += [Exchange("shift", distance, size), Exchange("shift", size - distance, size)]
        elif distance < REACH:
            swaps.append(Exchange("swap", distance, size, colour))
            others.insert(0, Exchange("other", distance, size))
        else:
            far += [Exchange("swap", distance, size, colour), Exchange("other", distance, size)]
    return swaps, shifts + others, far


def payload(exchange, pairs):
    return (pairs if exchange.colour is not None else 0) + (1 if exchange.listed else 0)


def when(condition, action):
    if condition is None:
        action()
    else:
        pl.when(condition)(action)


def split(value):
    high = value.astype(BF16)
    return high, (value - high.astype(F32)).astype(BF16)


def product(left, right):
    dot = functools.partial(jnp.dot, preferred_element_type=F32)
    return dot(left[0], right[0]) + (dot(left[0], right[1]) + dot(left[1], right[0]))


def outgoing_slots(exchange, me, mats, left_ref, count_ref, match_ref):
    slots = []
    if exchange.colour is not None:
        for j in range(match_ref.shape[2]):
            slots.append(match_ref[0, exchange.colour, j, 0])
    if exchange.listed:
        peer = exchange.peer(me, True)
        slot = jnp.int32(0)
        for j in range(left_ref.shape[1]):
            source = left_ref[1, j, peer]
            hit = (j < count_ref[peer]) & (lax.div(source, mats) == me)
            slot = jnp.where(hit, lax.rem(source, mats), slot)
        slots.append(slot)
    return slots


def incoming_rows(exchange, me, mats, left_ref, count_ref, match_ref, left_root, match_root, bath_ref):
    rows = []

    def row(live, target, mode, flag, root):
        lower = flag == 1
        a = jnp.where(lower, jnp.float32(1), bath_ref[0, mode])
        b = jnp.where(lower, jnp.float32(0), bath_ref[1, mode])
        rows.append((live, target, mode, a * root, b * root))

    if exchange.colour is not None:
        c = exchange.colour
        for j in range(match_ref.shape[2]):
            row(None, match_ref[0, c, j, 0], match_ref[0, c, j, 2], match_ref[0, c, j, 3], match_root[c, j])
    if exchange.listed:
        peer = exchange.peer(me, False)
        found = [jnp.int32(0)] * 4 + [jnp.float32(0)]
        for j in range(left_ref.shape[1]):
            hit = (j < count_ref[me]) & (lax.div(left_ref[1, j, me], mats) == peer)
            here = [1, left_ref[0, j, me], left_ref[2, j, me], left_ref[3, j, me], left_root[j, me]]
            found = [jnp.where(hit, new, old) for new, old in zip(here, found)]
        row(found[0] == 1, found[1], found[2], found[3], found[4])
    return rows


def pack_kernel(plan, mats, me_ref, left_ref, count_ref, match_ref, source, *rest):
    rest, (held, load_sems, sems) = rest[:-3], rest[-3:]
    sends = rest[len(rest) - len(plan) :]
    loads, stores = [], []
    for exchange, send in zip(plan, sends):
        slots = outgoing_slots(exchange, me_ref[0], mats, left_ref, count_ref, match_ref)
        for place, slot in enumerate(slots):
            at = len(loads)
            loads.append(pltpu.make_async_copy(source.at[slot], held.at[at], load_sems.at[at]))
            stores.append(pltpu.make_async_copy(held.at[at], send.at[place], sems.at[at]))
    for load in loads:
        load.start()
    for load, store in zip(loads, stores):
        load.wait()
        store.start()
    for store in stores:
        store.wait()


def commutator(density, hamiltonian):
    parts = []
    for part in (density[0], density[1]):
        halves = split(part)
        parts.append(product(hamiltonian, halves) - product(halves, hamiltonian))
    return parts[1], -parts[0]


def local_kernel(second, damping_ref, hamiltonian_ref, density_ref, *refs):
    out_ref = refs[-1]
    decay = damping_ref[pl.program_id(0)]
    density = (density_ref[0, 0], density_ref[0, 1])
    turned = commutator(density, split(hamiltonian_ref[...]))
    for part in range(2):
        slope = turned[part] - decay * density[part]
        if second:
            slope = refs[0][0, part] + STEP * density[part] + (0.5 * STEP * STEP) * slope
        out_ref[0, part] = slope


def local_call(damping, hamiltonian, *densities):
    mats, _, order, _ = densities[0].shape
    block = pl.BlockSpec((1, 2, order, order), lambda n: (n, 0, 0, 0))
    return pl.pallas_call(
        functools.partial(local_kernel, len(densities) == 2),
        grid=(mats,),
        in_specs=[SMEM, pl.BlockSpec((order, order), lambda n: (0, 0))] + [block] * len(densities),
        out_specs=block,
        out_shape=jax.ShapeDtypeStruct(densities[0].shape, F32),
        compiler_params=pltpu.CompilerParams(vmem_limit_bytes=GRANT),
        cost_estimate=pl.CostEstimate(
            flops=mats * 24 * order**3, bytes_accessed=mats * (1 + len(densities)) * 8 * order**2, transcendentals=0
        ),
    )(damping, hamiltonian, *densities)


def rows_kernel(plan, packs, scale, *refs):
    me_ref, left_ref, count_ref, match_ref, left_root, match_root, bath_ref, couplings_ref = refs[:8]
    arrivals = refs[8 : 8 + len(plan)]
    acc_in = refs[8 + len(plan)]
    rest = refs[9 + len(plan) :]
    acc_out, sends = rest[0], rest[1 : 1 + len(packs)]
    acc, landed, chosen, acc_sems, land_sems, mode_sems, send_sems = rest[1 + len(packs) :]
    mats, me = acc.shape[0], me_ref[0]
    rows, lands, modes = [], [], []
    for exchange, arrival in zip(plan, arrivals):
        found = incoming_rows(exchange, me, mats, left_ref, count_ref, match_ref, left_root, match_root, bath_ref)
        for place, row in enumerate(found):
            at = len(rows)
            lands.append(pltpu.make_async_copy(arrival.at[place], landed.at[at], land_sems.at[at]))
            modes.append(pltpu.make_async_copy(couplings_ref.at[row[2]], chosen.at[at], mode_sems.at[at]))
            rows.append(row)
    for (live, *_), land, mode in zip(rows, lands, modes):
        when(live, land.start)
        when(live, mode.start)

    def touches(n):
        return functools.reduce(
            jnp.logical_or, [row[1] == n if row[0] is None else row[0] & (row[1] == n) for row in rows]
        )

    touched = [touches(n) for n in range(mats)]
    loads = [pltpu.make_async_copy(acc_in.at[n], acc.at[n], acc_sems.at[n]) for n in range(mats)]
    stores = [pltpu.make_async_copy(acc.at[n], acc_out.at[n], acc_sems.at[n]) for n in range(mats)]
    for n in range(mats):
        when(None if packs else touched[n], loads[n].start)

    def loaded():
        for n in range(mats):
            when(None if packs else touched[n], loads[n].wait)
        for untouched, copy in early:
            when(untouched, copy.start)

    early, late, copies = [], [], []
    for exchange, send in zip(packs, sends):
        slots = outgoing_slots(exchange, me, mats, left_ref, count_ref, match_ref)
        for place, slot in enumerate(slots):
            copy = pltpu.make_async_copy(acc.at[slot], send.at[place], send_sems.at[len(copies)])
            busy = touches(slot)
            copies.append(copy)
            late.append((busy, copy))
            early.append((jnp.logical_not(busy), copy))
    if rows[0][0] is not None:
        loaded()
    for at, (live, target, _, a, b) in enumerate(rows):

        def add(at=at, target=target, a=a, b=b, first=at == 0 and live is None):
            modes[at].wait()
            lands[at].wait()
            coupling = split(chosen[at])
            real, imag = split(landed[at, 0]), split(landed[at, 1])
            left_re, right_re = product(coupling, real), product(real, coupling)
            left_im, right_im = product(coupling, imag), product(imag, coupling)
            edge_re = a * (left_re - right_re) - b * (left_im + right_im)
            edge_im = a * (left_im - right_im) + b * (left_re + right_re)
            if first:
                loaded()
            acc[target, 0] += scale * edge_im
            acc[target, 1] -= scale * edge_re

        when(live, add)
    for busy, copy in late:
        when(busy, copy.start)
    for n in range(mats):
        when(touched[n], stores[n].start)
    for copy in copies:
        copy.wait()
    for n in range(mats):
        when(touched[n], stores[n].wait)


def rows_call(plan, packs, pairs, scale, tables, couplings, arrivals, acc):
    mats, _, order, _ = acc.shape
    count = sum(payload(e, pairs) for e in plan)
    sent = sum(payload(e, pairs) for e in packs)
    shapes = [jax.ShapeDtypeStruct(acc.shape, F32)]
    shapes += [jax.ShapeDtypeStruct((payload(e, pairs), 2, order, order), F32) for e in packs]
    return pl.pallas_call(
        functools.partial(rows_kernel, plan, packs, scale),
        in_specs=[SMEM] * 7 + [HBM] + [ANY] * len(plan) + [HBM],
        out_specs=[HBM] * len(shapes),
        out_shape=shapes,
        input_output_aliases={8 + len(plan): 0},
        scratch_shapes=[
            pltpu.VMEM((mats, 2, order, order), F32),
            pltpu.VMEM((count, 2, order, order), F32),
            pltpu.VMEM((count, order, order), F32),
            pltpu.SemaphoreType.DMA((mats,)),
            pltpu.SemaphoreType.DMA((count,)),
            pltpu.SemaphoreType.DMA((count,)),
            pltpu.SemaphoreType.DMA((max(sent, 1),)),
        ],
        compiler_params=pltpu.CompilerParams(vmem_limit_bytes=GRANT),
        cost_estimate=pl.CostEstimate(
            flops=count * 24 * order**3, bytes_accessed=(count + 2 * mats + sent) * 8 * order**2, transcendentals=0
        ),
    )(*tables, couplings, *arrivals, acc)


def pack_call(plan, pairs, tables, source, *after):
    mats, _, order, _ = source.shape
    sent = sum(payload(e, pairs) for e in plan)
    return pl.pallas_call(
        functools.partial(pack_kernel, plan, mats),
        in_specs=[SMEM] * 4 + [HBM] + [ANY] * len(after),
        out_specs=[HBM] * len(plan),
        out_shape=[jax.ShapeDtypeStruct((payload(e, pairs), 2, order, order), F32) for e in plan],
        scratch_shapes=[
            pltpu.VMEM((sent, 2, order, order), F32),
            pltpu.SemaphoreType.DMA((sent,)),
            pltpu.SemaphoreType.DMA((sent,)),
        ],
        compiler_params=pltpu.CompilerParams(vmem_limit_bytes=GRANT),
        cost_estimate=pl.CostEstimate(flops=0, bytes_accessed=sent * 16 * order**2, transcendentals=0),
    )(*tables[:4], source, *after)


def body(rho, hamiltonian, couplings, bath_coef, damping, match_edges, left_rows, left_count):
    colours, pairs = match_edges.shape[1:3]
    swaps, shifts, far = exchanges(lax.axis_size("tier"), colours)
    me = lax.axis_index("tier").astype(jnp.int32)[None]
    left_fields = jnp.transpose(left_rows, (2, 1, 0))
    left_root = jnp.sqrt(left_fields[4].astype(F32))
    match_root = jnp.sqrt(match_edges[0, :, :, 4].astype(F32))
    tables = (me, left_fields, left_count, match_edges, left_root, match_root, bath_coef.T)

    near = swaps + shifts

    def gather(density, near_sends, acc, scale, packs):
        arrived = [e.permute(s) for e, s in zip(near, near_sends)]
        far_sends = pack_call(far, pairs, tables, density, *arrived[: len(swaps)])
        arrived += [e.permute(s) for e, s in zip(far, far_sends)]
        for group in (swaps, shifts, far):
            got = rows_call(
                group, packs if group is far else [], pairs, scale, tables, couplings, arrived[: len(group)], acc
            )
            acc, arrived = got[0], arrived[len(group) :]
        return acc, got[1:]

    sends = pack_call(near, pairs, tables, rho)
    first, sends = gather(rho, sends, local_call(damping, hamiltonian, rho), 1.0, near)
    return gather(first, sends, local_call(damping, hamiltonian, first, rho), 0.5 * STEP * STEP, [])[0]


def solution(mesh):
    placed = (
        P(("groups", "tier"), None, None, None),
        P(),
        P(),
        P("groups", None),
        P(("groups", "tier")),
        P("tier", None, None, None),
        P(),
        P(),
    )
    return jax.shard_map(
        body,
        mesh=mesh,
        in_specs=placed,
        out_specs=P(("groups", "tier"), None, None, None),
        check_vma=False,
    )
```

```python
import functools

import jax
import jax.numpy as jnp
from jax import lax
from jax.experimental import pallas as pl
from jax.experimental.pallas import tpu as pltpu
from jax.sharding import PartitionSpec as P

REACH = 4
STEP = 0.1
F32, BF16 = jnp.float32, jnp.bfloat16
SMEM = pl.BlockSpec(memory_space=pltpu.SMEM)
HBM = pl.BlockSpec(memory_space=pltpu.HBM)
ANY = pl.BlockSpec(memory_space=pl.ANY)
GRANT = 48 * 1024 * 1024


class Exchange:
    def __init__(self, kind, step, size, colour=None, listed=True):
        self.kind, self.step, self.size, self.colour, self.listed = kind, step, size, colour, listed

    def peer(self, index, outgoing):
        size, step = self.size, self.step
        if self.kind == "swap":
            return index ^ step
        if self.kind == "other":
            lower = (index & step) == 0
            if isinstance(index, int):
                return (index + (-step if lower else step)) % size
            return lax.rem(index + jnp.where(lower, size - step, step), size)
        move = step if outgoing else size - step
        if isinstance(index, int):
            return (index + move) % size
        return lax.rem(index + move, size)

    def permute(self, value):
        return lax.ppermute(value, "tier", [(i, self.peer(i, True)) for i in range(self.size)])


def exchanges(size, colours):
    shifts, others, swaps, far = [], [], [], []
    for distance in range(1, REACH + 1):
        colour = distance.bit_length() - 1
        if distance != 1 << colour or colour >= colours:
            shifts += [Exchange("shift", distance, size), Exchange("shift", size - distance, size)]
            continue
        swaps.append(Exchange("swap", distance, size, colour))
        (others if distance < REACH else far).insert(0, Exchange("other", distance, size))
    for colour in range(colours):
        if 1 << colour > REACH:
            far.insert(0, Exchange("swap", 1 << colour, size, colour, listed=False))
    return shifts, others, swaps, far


def payload(exchange, pairs):
    return (pairs if exchange.colour is not None else 0) + (1 if exchange.listed else 0)


def when(condition, action):
    if condition is None:
        action()
    else:
        pl.when(condition)(action)


def split(value):
    high = value.astype(BF16)
    return high, (value - high.astype(F32)).astype(BF16)


def product(left, right):
    dot = functools.partial(jnp.dot, preferred_element_type=F32)
    return dot(left[0], right[0]) + (dot(left[0], right[1]) + dot(left[1], right[0]))


def outgoing_slots(exchange, me, mats, left_ref, count_ref, match_ref):
    slots = []
    if exchange.colour is not None:
        for j in range(match_ref.shape[2]):
            slots.append(match_ref[0, exchange.colour, j, 0])
    if exchange.listed:
        peer = exchange.peer(me, True)
        slot = jnp.int32(0)
        for j in range(left_ref.shape[1]):
            source = left_ref[1, j, peer]
            hit = (j < count_ref[peer]) & (lax.div(source, mats) == me)
            slot = jnp.where(hit, lax.rem(source, mats), slot)
        slots.append(slot)
    return slots


def incoming_rows(exchange, me, mats, left_ref, count_ref, match_ref, left_root, match_root, bath_ref):
    rows = []

    def row(live, target, mode, flag, root):
        lower = flag == 1
        a = jnp.where(lower, jnp.float32(1), bath_ref[0, mode])
        b = jnp.where(lower, jnp.float32(0), bath_ref[1, mode])
        rows.append((live, target, mode, a * root, b * root))

    if exchange.colour is not None:
        c = exchange.colour
        for j in range(match_ref.shape[2]):
            row(None, match_ref[0, c, j, 0], match_ref[0, c, j, 2], match_ref[0, c, j, 3], match_root[c, j])
    if exchange.listed:
        peer = exchange.peer(me, False)
        found = [jnp.int32(0)] * 4 + [jnp.float32(0)]
        for j in range(left_ref.shape[1]):
            hit = (j < count_ref[me]) & (lax.div(left_ref[1, j, me], mats) == peer)
            here = [1, left_ref[0, j, me], left_ref[2, j, me], left_ref[3, j, me], left_root[j, me]]
            found = [jnp.where(hit, new, old) for new, old in zip(here, found)]
        row(found[0] == 1, found[1], found[2], found[3], found[4])
    return rows


def pack_kernel(plan, mats, me_ref, left_ref, count_ref, match_ref, source, *rest):
    rest, (held, load_sems, sems) = rest[:-3], rest[-3:]
    sends = rest[len(rest) - len(plan) :]
    loads, stores = [], []
    for exchange, send in zip(plan, sends):
        slots = outgoing_slots(exchange, me_ref[0], mats, left_ref, count_ref, match_ref)
        for place, slot in enumerate(slots):
            at = len(loads)
            loads.append(pltpu.make_async_copy(source.at[slot], held.at[at], load_sems.at[at]))
            stores.append(pltpu.make_async_copy(held.at[at], send.at[place], sems.at[at]))
    for load in loads:
        load.start()
    for load, store in zip(loads, stores):
        load.wait()
        store.start()
    for store in stores:
        store.wait()


def commutator(density, hamiltonian):
    parts = []
    for part in (density[0], density[1]):
        halves = split(part)
        parts.append(product(hamiltonian, halves) - product(halves, hamiltonian))
    return parts[1], -parts[0]


def local_kernel(second, damping_ref, hamiltonian_ref, density_ref, *refs):
    out_ref = refs[-1]
    decay = damping_ref[pl.program_id(0)]
    density = (density_ref[0, 0], density_ref[0, 1])
    turned = commutator(density, split(hamiltonian_ref[...]))
    for part in range(2):
        slope = turned[part] - decay * density[part]
        if second:
            slope = refs[0][0, part] + STEP * density[part] + (0.5 * STEP * STEP) * slope
        out_ref[0, part] = slope


def local_call(damping, hamiltonian, *densities):
    mats, _, order, _ = densities[0].shape
    block = pl.BlockSpec((1, 2, order, order), lambda n: (n, 0, 0, 0))
    return pl.pallas_call(
        functools.partial(local_kernel, len(densities) == 2),
        grid=(mats,),
        in_specs=[SMEM, pl.BlockSpec((order, order), lambda n: (0, 0))] + [block] * len(densities),
        out_specs=block,
        out_shape=jax.ShapeDtypeStruct(densities[0].shape, F32),
        compiler_params=pltpu.CompilerParams(vmem_limit_bytes=GRANT),
        cost_estimate=pl.CostEstimate(
            flops=mats * 24 * order**3, bytes_accessed=mats * (1 + len(densities)) * 8 * order**2, transcendentals=0
        ),
    )(damping, hamiltonian, *densities)


def rows_kernel(plan, packs, scale, *refs):
    me_ref, left_ref, count_ref, match_ref, left_root, match_root, bath_ref, couplings_ref = refs[:8]
    arrivals = refs[8 : 8 + len(plan)]
    acc_in = refs[8 + len(plan)]
    rest = refs[9 + len(plan) :]
    acc_out, sends = rest[0], rest[1 : 1 + len(packs)]
    acc, landed, chosen, acc_sems, land_sems, mode_sems, send_sems = rest[1 + len(packs) :]
    mats, me = acc.shape[0], me_ref[0]
    rows, lands, modes = [], [], []
    for exchange, arrival in zip(plan, arrivals):
        found = incoming_rows(exchange, me, mats, left_ref, count_ref, match_ref, left_root, match_root, bath_ref)
        for place, row in enumerate(found):
            at = len(rows)
            lands.append(pltpu.make_async_copy(arrival.at[place], landed.at[at], land_sems.at[at]))
            modes.append(pltpu.make_async_copy(couplings_ref.at[row[2]], chosen.at[at], mode_sems.at[at]))
            rows.append(row)
    for (live, *_), land, mode in zip(rows, lands, modes):
        when(live, land.start)
        when(live, mode.start)

    def touches(n):
        return functools.reduce(
            jnp.logical_or, [row[1] == n if row[0] is None else row[0] & (row[1] == n) for row in rows]
        )

    touched = [touches(n) for n in range(mats)]
    loads = [pltpu.make_async_copy(acc_in.at[n], acc.at[n], acc_sems.at[n]) for n in range(mats)]
    stores = [pltpu.make_async_copy(acc.at[n], acc_out.at[n], acc_sems.at[n]) for n in range(mats)]
    for n in range(mats):
        when(None if packs else touched[n], loads[n].start)

    def loaded():
        for n in range(mats):
            when(None if packs else touched[n], loads[n].wait)
        for untouched, copy in early:
            when(untouched, copy.start)

    early, late, copies = [], [], []
    for exchange, send in zip(packs, sends):
        slots = outgoing_slots(exchange, me, mats, left_ref, count_ref, match_ref)
        for place, slot in enumerate(slots):
            copy = pltpu.make_async_copy(acc.at[slot], send.at[place], send_sems.at[len(copies)])
            busy = touches(slot)
            copies.append(copy)
            late.append((busy, copy))
            early.append((jnp.logical_not(busy), copy))
    if rows[0][0] is not None:
        loaded()
    for at, (live, target, _, a, b) in enumerate(rows):

        def add(at=at, target=target, a=a, b=b, first=at == 0 and live is None):
            modes[at].wait()
            lands[at].wait()
            coupling = split(chosen[at])
            real, imag = split(landed[at, 0]), split(landed[at, 1])
            left_re, right_re = product(coupling, real), product(real, coupling)
            left_im, right_im = product(coupling, imag), product(imag, coupling)
            edge_re = a * (left_re - right_re) - b * (left_im + right_im)
            edge_im = a * (left_im - right_im) + b * (left_re + right_re)
            if first:
                loaded()
            acc[target, 0] += scale * edge_im
            acc[target, 1] -= scale * edge_re

        when(live, add)
    for busy, copy in late:
        when(busy, copy.start)
    for n in range(mats):
        when(touched[n], stores[n].start)
    for copy in copies:
        copy.wait()
    for n in range(mats):
        when(touched[n], stores[n].wait)


def rows_call(plan, packs, pairs, scale, tables, couplings, arrivals, acc):
    mats, _, order, _ = acc.shape
    count = sum(payload(e, pairs) for e in plan)
    sent = sum(payload(e, pairs) for e in packs)
    shapes = [jax.ShapeDtypeStruct(acc.shape, F32)]
    shapes += [jax.ShapeDtypeStruct((payload(e, pairs), 2, order, order), F32) for e in packs]
    return pl.pallas_call(
        functools.partial(rows_kernel, plan, packs, scale),
        in_specs=[SMEM] * 7 + [HBM] + [ANY] * len(plan) + [HBM],
        out_specs=[HBM] * len(shapes),
        out_shape=shapes,
        input_output_aliases={8 + len(plan): 0},
        scratch_shapes=[
            pltpu.VMEM((mats, 2, order, order), F32),
            pltpu.VMEM((count, 2, order, order), F32),
            pltpu.VMEM((count, order, order), F32),
            pltpu.SemaphoreType.DMA((mats,)),
            pltpu.SemaphoreType.DMA((count,)),
            pltpu.SemaphoreType.DMA((count,)),
            pltpu.SemaphoreType.DMA((max(sent, 1),)),
        ],
        compiler_params=pltpu.CompilerParams(vmem_limit_bytes=GRANT),
        cost_estimate=pl.CostEstimate(
            flops=count * 24 * order**3, bytes_accessed=(count + 2 * mats + sent) * 8 * order**2, transcendentals=0
        ),
    )(*tables, couplings, *arrivals, acc)


def pack_call(plan, pairs, tables, source, *after):
    mats, _, order, _ = source.shape
    sent = sum(payload(e, pairs) for e in plan)
    return pl.pallas_call(
        functools.partial(pack_kernel, plan, mats),
        in_specs=[SMEM] * 4 + [HBM] + [ANY] * len(after),
        out_specs=[HBM] * len(plan),
        out_shape=[jax.ShapeDtypeStruct((payload(e, pairs), 2, order, order), F32) for e in plan],
        scratch_shapes=[
            pltpu.VMEM((sent, 2, order, order), F32),
            pltpu.SemaphoreType.DMA((sent,)),
            pltpu.SemaphoreType.DMA((sent,)),
        ],
        compiler_params=pltpu.CompilerParams(vmem_limit_bytes=GRANT),
        cost_estimate=pl.CostEstimate(flops=0, bytes_accessed=sent * 16 * order**2, transcendentals=0),
    )(*tables[:4], source, *after)


def body(rho, hamiltonian, couplings, bath_coef, damping, match_edges, left_rows, left_count):
    colours, pairs = match_edges.shape[1:3]
    shifts, others, swaps, far = exchanges(lax.axis_size("tier"), colours)
    me = lax.axis_index("tier").astype(jnp.int32)[None]
    left_fields = jnp.transpose(left_rows, (2, 1, 0))
    left_root = jnp.sqrt(left_fields[4].astype(F32))
    match_root = jnp.sqrt(match_edges[0, :, :, 4].astype(F32))
    tables = (me, left_fields, left_count, match_edges, left_root, match_root, bath_coef.T)

    near, later = shifts + others + swaps[:1], swaps[1:] + far

    def gather(density, near_sends, acc, scale, packs):
        arrived = [e.permute(s) for e, s in zip(near, near_sends)]
        sends = pack_call(later, pairs, tables, density, *arrived[: len(shifts)])
        arrived += [e.permute(s) for e, s in zip(later, sends)]
        first, second = len(shifts + others), len(near) + 1
        order = near + later
        for a, b in ((0, first), (first, second), (second, len(order))):
            got = rows_call(
                order[a:b], packs if b == len(order) else [], pairs, scale, tables, couplings, arrived[a:b], acc
            )
            acc = got[0]
        return acc, got[1:]

    sends = pack_call(near, pairs, tables, rho)
    first, sends = gather(rho, sends, local_call(damping, hamiltonian, rho), 1.0, near)
    return gather(first, sends, local_call(damping, hamiltonian, first, rho), 0.5 * STEP * STEP, [])[0]


def solution(mesh):
    placed = (
        P(("groups", "tier"), None, None, None),
        P(),
        P(),
        P("groups", None),
        P(("groups", "tier")),
        P("tier", None, None, None),
        P(),
        P(),
    )
    return jax.shard_map(
        body,
        mesh=mesh,
        in_specs=placed,
        out_specs=P(("groups", "tier"), None, None, None),
        check_vma=False,
    )
```

```python
import functools

import jax
import jax.numpy as jnp
from jax import lax
from jax.experimental import pallas as pl
from jax.experimental.pallas import tpu as pltpu
from jax.sharding import PartitionSpec as P

REACH = 4
STEP = 0.1
F32, BF16 = jnp.float32, jnp.bfloat16
SMEM = pl.BlockSpec(memory_space=pltpu.SMEM)
HBM = pl.BlockSpec(memory_space=pltpu.HBM)
ANY = pl.BlockSpec(memory_space=pl.ANY)
GRANT = 48 * 1024 * 1024


class Exchange:
    def __init__(self, kind, step, size, colour=None, listed=True):
        self.kind, self.step, self.size, self.colour, self.listed = kind, step, size, colour, listed

    def peer(self, index, outgoing):
        size, step = self.size, self.step
        if self.kind == "swap":
            return index ^ step
        if self.kind == "other":
            lower = (index & step) == 0
            if isinstance(index, int):
                return (index + (-step if lower else step)) % size
            return lax.rem(index + jnp.where(lower, size - step, step), size)
        move = step if outgoing else size - step
        if isinstance(index, int):
            return (index + move) % size
        return lax.rem(index + move, size)

    def permute(self, value):
        return lax.ppermute(value, "tier", [(i, self.peer(i, True)) for i in range(self.size)])


def exchanges(size, colours):
    shifts, others, swaps, far = [], [], [], []
    for distance in range(1, REACH + 1):
        colour = distance.bit_length() - 1
        if distance != 1 << colour or colour >= colours:
            shifts += [Exchange("shift", distance, size), Exchange("shift", size - distance, size)]
            continue
        swaps.append(Exchange("swap", distance, size, colour))
        (others if distance < REACH else far).insert(0, Exchange("other", distance, size))
    for colour in range(colours):
        if 1 << colour > REACH:
            swaps.insert(1, Exchange("swap", 1 << colour, size, colour, listed=False))
    return shifts + others + swaps[:1], swaps[1:] + far


def payload(exchange, pairs):
    return (pairs if exchange.colour is not None else 0) + (1 if exchange.listed else 0)


def when(condition, action):
    if condition is None:
        action()
    else:
        pl.when(condition)(action)


def split(value):
    high = value.astype(BF16)
    return high, (value - high.astype(F32)).astype(BF16)


def product(left, right):
    dot = functools.partial(jnp.dot, preferred_element_type=F32)
    return dot(left[0], right[0]) + (dot(left[0], right[1]) + dot(left[1], right[0]))


def outgoing_slots(exchange, me, mats, left_ref, count_ref, match_ref):
    slots = []
    if exchange.colour is not None:
        for j in range(match_ref.shape[2]):
            slots.append(match_ref[0, exchange.colour, j, 0])
    if exchange.listed:
        peer = exchange.peer(me, True)
        slot = jnp.int32(0)
        for j in range(left_ref.shape[1]):
            source = left_ref[1, j, peer]
            hit = (j < count_ref[peer]) & (lax.div(source, mats) == me)
            slot = jnp.where(hit, lax.rem(source, mats), slot)
        slots.append(slot)
    return slots


def incoming_rows(exchange, me, mats, left_ref, count_ref, match_ref, left_root, match_root, bath_ref):
    rows = []

    def row(live, target, mode, flag, root):
        lower = flag == 1
        a = jnp.where(lower, jnp.float32(1), bath_ref[0, mode])
        b = jnp.where(lower, jnp.float32(0), bath_ref[1, mode])
        rows.append((live, target, mode, a * root, b * root))

    if exchange.colour is not None:
        c = exchange.colour
        for j in range(match_ref.shape[2]):
            row(None, match_ref[0, c, j, 0], match_ref[0, c, j, 2], match_ref[0, c, j, 3], match_root[c, j])
    if exchange.listed:
        peer = exchange.peer(me, False)
        found = [jnp.int32(0)] * 4 + [jnp.float32(0)]
        for j in range(left_ref.shape[1]):
            hit = (j < count_ref[me]) & (lax.div(left_ref[1, j, me], mats) == peer)
            here = [1, left_ref[0, j, me], left_ref[2, j, me], left_ref[3, j, me], left_root[j, me]]
            found = [jnp.where(hit, new, old) for new, old in zip(here, found)]
        row(found[0] == 1, found[1], found[2], found[3], found[4])
    return rows


def pack_kernel(plan, mats, me_ref, left_ref, count_ref, match_ref, source, *rest):
    sends, (held, load_sems, sems) = rest[:-3], rest[-3:]
    loads, stores = [], []
    for exchange, send in zip(plan, sends):
        slots = outgoing_slots(exchange, me_ref[0], mats, left_ref, count_ref, match_ref)
        for place, slot in enumerate(slots):
            at = len(loads)
            loads.append(pltpu.make_async_copy(source.at[slot], held.at[at], load_sems.at[at]))
            stores.append(pltpu.make_async_copy(held.at[at], send.at[place], sems.at[at]))
    for load in loads:
        load.start()
    for load, store in zip(loads, stores):
        load.wait()
        store.start()
    for store in stores:
        store.wait()


def commutator(density, hamiltonian):
    parts = []
    for part in (density[0], density[1]):
        halves = split(part)
        parts.append(product(hamiltonian, halves) - product(halves, hamiltonian))
    return parts[1], -parts[0]


def local_kernel(second, damping_ref, hamiltonian_ref, density_ref, *refs):
    out_ref = refs[-1]
    decay = damping_ref[pl.program_id(0)]
    density = (density_ref[0, 0], density_ref[0, 1])
    turned = commutator(density, split(hamiltonian_ref[...]))
    for part in range(2):
        slope = turned[part] - decay * density[part]
        if second:
            slope = refs[0][0, part] + STEP * density[part] + (0.5 * STEP * STEP) * slope
        out_ref[0, part] = slope


def local_call(damping, hamiltonian, *densities):
    mats, _, order, _ = densities[0].shape
    block = pl.BlockSpec((1, 2, order, order), lambda n: (n, 0, 0, 0))
    return pl.pallas_call(
        functools.partial(local_kernel, len(densities) == 2),
        grid=(mats,),
        in_specs=[SMEM, pl.BlockSpec((order, order), lambda n: (0, 0))] + [block] * len(densities),
        out_specs=block,
        out_shape=jax.ShapeDtypeStruct(densities[0].shape, F32),
        compiler_params=pltpu.CompilerParams(vmem_limit_bytes=GRANT),
        cost_estimate=pl.CostEstimate(
            flops=mats * 24 * order**3, bytes_accessed=mats * (1 + len(densities)) * 8 * order**2, transcendentals=0
        ),
    )(damping, hamiltonian, *densities)


def rows_kernel(plan, packs, scale, *refs):
    me_ref, left_ref, count_ref, match_ref, left_root, match_root, bath_ref, couplings_ref = refs[:8]
    arrivals = refs[8 : 8 + len(plan)]
    acc_in = refs[8 + len(plan)]
    rest = refs[9 + len(plan) :]
    acc_out, sends = rest[0], rest[1 : 1 + len(packs)]
    acc, landed, chosen, acc_sems, land_sems, mode_sems, send_sems = rest[1 + len(packs) :]
    mats, me = acc.shape[0], me_ref[0]
    rows, lands, modes = [], [], []
    for exchange, arrival in zip(plan, arrivals):
        found = incoming_rows(exchange, me, mats, left_ref, count_ref, match_ref, left_root, match_root, bath_ref)
        for place, row in enumerate(found):
            at = len(rows)
            lands.append(pltpu.make_async_copy(arrival.at[place], landed.at[at], land_sems.at[at]))
            modes.append(pltpu.make_async_copy(couplings_ref.at[row[2]], chosen.at[at], mode_sems.at[at]))
            rows.append(row)
    for (live, *_), land, mode in zip(rows, lands, modes):
        when(live, land.start)
        when(live, mode.start)

    def touches(n):
        return functools.reduce(
            jnp.logical_or, [row[1] == n if row[0] is None else row[0] & (row[1] == n) for row in rows]
        )

    touched = [touches(n) for n in range(mats)]
    loads = [pltpu.make_async_copy(acc_in.at[n], acc.at[n], acc_sems.at[n]) for n in range(mats)]
    stores = [pltpu.make_async_copy(acc.at[n], acc_out.at[n], acc_sems.at[n]) for n in range(mats)]
    for n in range(mats):
        when(None if packs else touched[n], loads[n].start)

    def loaded():
        for n in range(mats):
            when(None if packs else touched[n], loads[n].wait)
        for untouched, copy in early:
            when(untouched, copy.start)

    early, late, copies = [], [], []
    for exchange, send in zip(packs, sends):
        slots = outgoing_slots(exchange, me, mats, left_ref, count_ref, match_ref)
        for place, slot in enumerate(slots):
            copy = pltpu.make_async_copy(acc.at[slot], send.at[place], send_sems.at[len(copies)])
            busy = touches(slot)
            copies.append(copy)
            late.append((busy, copy))
            early.append((jnp.logical_not(busy), copy))
    if rows[0][0] is not None:
        loaded()
    for at, (live, target, _, a, b) in enumerate(rows):

        def add(at=at, target=target, a=a, b=b, first=at == 0 and live is None):
            modes[at].wait()
            lands[at].wait()
            coupling = split(chosen[at])
            real, imag = split(landed[at, 0]), split(landed[at, 1])
            left_re, right_re = product(coupling, real), product(real, coupling)
            left_im, right_im = product(coupling, imag), product(imag, coupling)
            edge_re = a * (left_re - right_re) - b * (left_im + right_im)
            edge_im = a * (left_im - right_im) + b * (left_re + right_re)
            if first:
                loaded()
            acc[target, 0] += scale * edge_im
            acc[target, 1] -= scale * edge_re

        when(live, add)
    for busy, copy in late:
        when(busy, copy.start)
    for n in range(mats):
        when(touched[n], stores[n].start)
    for copy in copies:
        copy.wait()
    for n in range(mats):
        when(touched[n], stores[n].wait)


def rows_call(plan, packs, pairs, scale, tables, couplings, arrivals, acc):
    mats, _, order, _ = acc.shape
    count = sum(payload(e, pairs) for e in plan)
    sent = sum(payload(e, pairs) for e in packs)
    shapes = [jax.ShapeDtypeStruct(acc.shape, F32)]
    shapes += [jax.ShapeDtypeStruct((payload(e, pairs), 2, order, order), F32) for e in packs]
    return pl.pallas_call(
        functools.partial(rows_kernel, plan, packs, scale),
        in_specs=[SMEM] * 7 + [HBM] + [ANY] * len(plan) + [HBM],
        out_specs=[HBM] * len(shapes),
        out_shape=shapes,
        input_output_aliases={8 + len(plan): 0},
        scratch_shapes=[
            pltpu.VMEM((mats, 2, order, order), F32),
            pltpu.VMEM((count, 2, order, order), F32),
            pltpu.VMEM((count, order, order), F32),
            pltpu.SemaphoreType.DMA((mats,)),
            pltpu.SemaphoreType.DMA((count,)),
            pltpu.SemaphoreType.DMA((count,)),
            pltpu.SemaphoreType.DMA((max(sent, 1),)),
        ],
        compiler_params=pltpu.CompilerParams(vmem_limit_bytes=GRANT),
        cost_estimate=pl.CostEstimate(
            flops=count * 24 * order**3, bytes_accessed=(count + 2 * mats + sent) * 8 * order**2, transcendentals=0
        ),
    )(*tables, couplings, *arrivals, acc)


def pack_call(plan, pairs, tables, source):
    mats, _, order, _ = source.shape
    sent = sum(payload(e, pairs) for e in plan)
    return pl.pallas_call(
        functools.partial(pack_kernel, plan, mats),
        in_specs=[SMEM] * 4 + [HBM],
        out_specs=[HBM] * len(plan),
        out_shape=[jax.ShapeDtypeStruct((payload(e, pairs), 2, order, order), F32) for e in plan],
        scratch_shapes=[
            pltpu.VMEM((sent, 2, order, order), F32),
            pltpu.SemaphoreType.DMA((sent,)),
            pltpu.SemaphoreType.DMA((sent,)),
        ],
        compiler_params=pltpu.CompilerParams(vmem_limit_bytes=GRANT),
        cost_estimate=pl.CostEstimate(flops=0, bytes_accessed=sent * 16 * order**2, transcendentals=0),
    )(*tables[:4], source)


def body(rho, hamiltonian, couplings, bath_coef, damping, match_edges, left_rows, left_count):
    colours, pairs = match_edges.shape[1:3]
    early, late = exchanges(lax.axis_size("tier"), colours)
    me = lax.axis_index("tier").astype(jnp.int32)[None]
    left_fields = jnp.transpose(left_rows, (2, 1, 0))
    left_root = jnp.sqrt(left_fields[4].astype(F32))
    match_root = jnp.sqrt(match_edges[0, :, :, 4].astype(F32))
    tables = (me, left_fields, left_count, match_edges, left_root, match_root, bath_coef.T)

    plan = early + late

    def gather(sends, acc, scale, packs):
        arrived = [e.permute(s) for e, s in zip(plan, sends)]
        cut = len(early)
        acc = rows_call(early, [], pairs, scale, tables, couplings, arrived[:cut], acc)[0]
        acc, *sends = rows_call(late, packs, pairs, scale, tables, couplings, arrived[cut:], acc)
        return acc, sends

    sends = pack_call(plan, pairs, tables, rho)
    first, sends = gather(sends, local_call(damping, hamiltonian, rho), 1.0, plan)
    return gather(sends, local_call(damping, hamiltonian, first, rho), 0.5 * STEP * STEP, [])[0]


def solution(mesh):
    placed = (
        P(("groups", "tier"), None, None, None),
        P(),
        P(),
        P("groups", None),
        P(("groups", "tier")),
        P("tier", None, None, None),
        P(),
        P(),
    )
    return jax.shard_map(
        body,
        mesh=mesh,
        in_specs=placed,
        out_specs=P(("groups", "tier"), None, None, None),
        check_vma=False,
    )
```

```python
import functools

import jax
import jax.numpy as jnp
from jax import lax
from jax.experimental import pallas as pl
from jax.experimental.pallas import tpu as pltpu
from jax.sharding import PartitionSpec as P

REACH = 4
STEP = 0.1
F32, BF16 = jnp.float32, jnp.bfloat16
SMEM = pl.BlockSpec(memory_space=pltpu.SMEM)
HBM = pl.BlockSpec(memory_space=pltpu.HBM)
ANY = pl.BlockSpec(memory_space=pl.ANY)
GRANT = 24 * 1024 * 1024


class Exchange:
    def __init__(self, kind, step, size, colour=None, listed=True):
        self.kind, self.step, self.size, self.colour, self.listed = kind, step, size, colour, listed

    def peer(self, index, outgoing):
        size, step = self.size, self.step
        if self.kind == "swap":
            return index ^ step
        if self.kind == "other":
            lower = (index & step) == 0
            if isinstance(index, int):
                return (index + (-step if lower else step)) % size
            return lax.rem(index + jnp.where(lower, size - step, step), size)
        move = step if outgoing else size - step
        if isinstance(index, int):
            return (index + move) % size
        return lax.rem(index + move, size)

    def permute(self, value):
        return lax.ppermute(value, "tier", [(i, self.peer(i, True)) for i in range(self.size)])


def exchanges(size, colours):
    shifts, others, swaps, far = [], [], [], []
    for distance in range(1, REACH + 1):
        colour = distance.bit_length() - 1
        if distance != 1 << colour or colour >= colours:
            shifts += [Exchange("shift", distance, size), Exchange("shift", size - distance, size)]
            continue
        swaps.append(Exchange("swap", distance, size, colour))
        (others if distance < REACH else far).insert(0, Exchange("other", distance, size))
    for colour in range(colours):
        if 1 << colour > REACH:
            swaps.insert(1, Exchange("swap", 1 << colour, size, colour, listed=False))
    return shifts + others + swaps[:1], swaps[1:] + far


def payload(exchange, pairs):
    return (pairs if exchange.colour is not None else 0) + (1 if exchange.listed else 0)


def when(condition, action):
    if condition is None:
        action()
    else:
        pl.when(condition)(action)


def split(value):
    high = value.astype(BF16)
    return high, (value - high.astype(F32)).astype(BF16)


def product(left, right):
    dot = functools.partial(jnp.dot, preferred_element_type=F32)
    return dot(left[0], right[0]) + (dot(left[0], right[1]) + dot(left[1], right[0]))


def outgoing_slots(exchange, me, mats, left_ref, match_ref):
    slots = []
    if exchange.colour is not None:
        for j in range(match_ref.shape[2]):
            slots.append(match_ref[0, exchange.colour, j, 0])
    if exchange.listed:
        peer = exchange.peer(me, True)
        slot = jnp.int32(0)
        for j in reversed(range(left_ref.shape[1])):
            source = left_ref[1, j, peer]
            slot = jnp.where(lax.div(source, mats) == me, lax.rem(source, mats), slot)
        slots.append(slot)
    return slots


def incoming_rows(exchange, me, mats, left_ref, count_ref, match_ref, left_root, match_root, bath_ref):
    rows = []

    def row(live, target, mode, flag, root):
        lower = flag == 1
        a = jnp.where(lower, jnp.float32(1), bath_ref[0, mode])
        b = jnp.where(lower, jnp.float32(0), bath_ref[1, mode])
        rows.append((live, target, mode, a * root, b * root))

    if exchange.colour is not None:
        c = exchange.colour
        for j in range(match_ref.shape[2]):
            row(None, match_ref[0, c, j, 0], match_ref[0, c, j, 2], match_ref[0, c, j, 3], match_root[c, j])
    if exchange.listed:
        peer = exchange.peer(me, False)
        found = [jnp.int32(0)] * 4 + [jnp.float32(0)]
        for j in range(left_ref.shape[1]):
            hit = (j < count_ref[me]) & (lax.div(left_ref[1, j, me], mats) == peer)
            here = [1, left_ref[0, j, me], left_ref[2, j, me], left_ref[3, j, me], left_root[j, me]]
            found = [jnp.where(hit, new, old) for new, old in zip(here, found)]
        row(found[0] == 1, found[1], found[2], found[3], found[4])
    return rows


def pack_kernel(plan, mats, me_ref, left_ref, match_ref, source, *rest):
    sends, (held, load_sems, sems) = rest[:-3], rest[-3:]
    loads, stores = [], []
    for exchange, send in zip(plan, sends):
        slots = outgoing_slots(exchange, me_ref[0], mats, left_ref, match_ref)
        for place, slot in enumerate(slots):
            at = len(loads)
            loads.append(pltpu.make_async_copy(source.at[slot], held.at[at], load_sems.at[at]))
            stores.append(pltpu.make_async_copy(held.at[at], send.at[place], sems.at[at]))
    for load in loads:
        load.start()
    for load, store in zip(loads, stores):
        load.wait()
        store.start()
    for store in stores:
        store.wait()


def commutator(density, hamiltonian):
    parts = []
    for part in (density[0], density[1]):
        halves = split(part)
        parts.append(product(hamiltonian, halves) - product(halves, hamiltonian))
    return parts[1], -parts[0]


def local_kernel(second, damping_ref, hamiltonian_ref, density_ref, *refs):
    out_ref = refs[-1]
    decay = damping_ref[pl.program_id(0)]
    density = (density_ref[0, 0], density_ref[0, 1])
    turned = commutator(density, split(hamiltonian_ref[...]))
    for part in range(2):
        slope = turned[part] - decay * density[part]
        if second:
            slope = refs[0][0, part] + STEP * density[part] + (0.5 * STEP * STEP) * slope
        out_ref[0, part] = slope


def local_call(damping, hamiltonian, *densities):
    mats, _, order, _ = densities[0].shape
    block = pl.BlockSpec((1, 2, order, order), lambda n: (n, 0, 0, 0))
    return pl.pallas_call(
        functools.partial(local_kernel, len(densities) == 2),
        grid=(mats,),
        in_specs=[SMEM, pl.BlockSpec((order, order), lambda n: (0, 0))] + [block] * len(densities),
        out_specs=block,
        out_shape=jax.ShapeDtypeStruct(densities[0].shape, F32),
        compiler_params=pltpu.CompilerParams(vmem_limit_bytes=GRANT),
        cost_estimate=pl.CostEstimate(
            flops=mats * 24 * order**3, bytes_accessed=mats * (1 + len(densities)) * 8 * order**2, transcendentals=0
        ),
    )(damping, hamiltonian, *densities)


def rows_kernel(plan, packs, scale, *refs):
    me_ref, left_ref, count_ref, match_ref, left_root, match_root, bath_ref, couplings_ref = refs[:8]
    arrivals = refs[8 : 8 + len(plan)]
    acc_in = refs[8 + len(plan)]
    rest = refs[9 + len(plan) :]
    acc_out, sends = rest[0], rest[1 : 1 + len(packs)]
    acc, landed, chosen, acc_sems, land_sems, mode_sems, send_sems = rest[1 + len(packs) :]
    mats, me = acc.shape[0], me_ref[0]
    rows, lands, modes = [], [], []
    for exchange, arrival in zip(plan, arrivals):
        found = incoming_rows(exchange, me, mats, left_ref, count_ref, match_ref, left_root, match_root, bath_ref)
        for place, row in enumerate(found):
            at = len(rows)
            lands.append(pltpu.make_async_copy(arrival.at[place], landed.at[at], land_sems.at[at]))
            modes.append(pltpu.make_async_copy(couplings_ref.at[row[2]], chosen.at[at], mode_sems.at[at]))
            rows.append(row)
    for (live, *_), land, mode in zip(rows, lands, modes):
        when(live, land.start)
        when(live, mode.start)

    def touches(n):
        return functools.reduce(
            jnp.logical_or, [row[1] == n if row[0] is None else row[0] & (row[1] == n) for row in rows]
        )

    touched = [touches(n) for n in range(mats)]
    loads = [pltpu.make_async_copy(acc_in.at[n], acc.at[n], acc_sems.at[n]) for n in range(mats)]
    stores = [pltpu.make_async_copy(acc.at[n], acc_out.at[n], acc_sems.at[n]) for n in range(mats)]
    for n in range(mats):
        when(None if packs else touched[n], loads[n].start)

    def loaded():
        for n in range(mats):
            when(None if packs else touched[n], loads[n].wait)
        for untouched, copy in early:
            when(untouched, copy.start)

    early, late, copies = [], [], []
    for exchange, send in zip(packs, sends):
        slots = outgoing_slots(exchange, me, mats, left_ref, match_ref)
        for place, slot in enumerate(slots):
            copy = pltpu.make_async_copy(acc.at[slot], send.at[place], send_sems.at[len(copies)])
            busy = touches(slot)
            copies.append(copy)
            late.append((busy, copy))
            early.append((jnp.logical_not(busy), copy))
    if rows[0][0] is not None:
        loaded()
    for at, (live, target, _, a, b) in enumerate(rows):

        def add(at=at, target=target, a=a, b=b, first=at == 0 and live is None):
            modes[at].wait()
            lands[at].wait()
            coupling = split(chosen[at])
            real, imag = split(landed[at, 0]), split(landed[at, 1])
            left_re, right_re = product(coupling, real), product(real, coupling)
            left_im, right_im = product(coupling, imag), product(imag, coupling)
            edge_re = a * (left_re - right_re) - b * (left_im + right_im)
            edge_im = a * (left_im - right_im) + b * (left_re + right_re)
            if first:
                loaded()
            acc[target, 0] += scale * edge_im
            acc[target, 1] -= scale * edge_re

        when(live, add)
    for busy, copy in late:
        when(busy, copy.start)
    for n in range(mats):
        when(touched[n], stores[n].start)
    for copy in copies:
        copy.wait()
    for n in range(mats):
        when(touched[n], stores[n].wait)


def rows_call(plan, packs, pairs, scale, tables, couplings, arrivals, acc):
    mats, _, order, _ = acc.shape
    count = sum(payload(e, pairs) for e in plan)
    sent = sum(payload(e, pairs) for e in packs)
    shapes = [jax.ShapeDtypeStruct(acc.shape, F32)]
    shapes += [jax.ShapeDtypeStruct((payload(e, pairs), 2, order, order), F32) for e in packs]
    return pl.pallas_call(
        functools.partial(rows_kernel, plan, packs, scale),
        in_specs=[SMEM] * 7 + [HBM] + [ANY] * len(plan) + [HBM],
        out_specs=[HBM] * len(shapes),
        out_shape=shapes,
        input_output_aliases={8 + len(plan): 0},
        scratch_shapes=[
            pltpu.VMEM((mats, 2, order, order), F32),
            pltpu.VMEM((count, 2, order, order), F32),
            pltpu.VMEM((count, order, order), F32),
            pltpu.SemaphoreType.DMA((mats,)),
            pltpu.SemaphoreType.DMA((count,)),
            pltpu.SemaphoreType.DMA((count,)),
            pltpu.SemaphoreType.DMA((max(sent, 1),)),
        ],
        compiler_params=pltpu.CompilerParams(vmem_limit_bytes=GRANT),
        cost_estimate=pl.CostEstimate(
            flops=count * 24 * order**3, bytes_accessed=(count + 2 * mats + sent) * 8 * order**2, transcendentals=0
        ),
    )(*tables, couplings, *arrivals, acc)


def pack_call(plan, pairs, tables, source):
    mats, _, order, _ = source.shape
    sent = sum(payload(e, pairs) for e in plan)
    return pl.pallas_call(
        functools.partial(pack_kernel, plan, mats),
        in_specs=[SMEM] * 3 + [HBM],
        out_specs=[HBM] * len(plan),
        out_shape=[jax.ShapeDtypeStruct((payload(e, pairs), 2, order, order), F32) for e in plan],
        scratch_shapes=[
            pltpu.VMEM((sent, 2, order, order), F32),
            pltpu.SemaphoreType.DMA((sent,)),
            pltpu.SemaphoreType.DMA((sent,)),
        ],
        compiler_params=pltpu.CompilerParams(vmem_limit_bytes=GRANT),
        cost_estimate=pl.CostEstimate(flops=0, bytes_accessed=sent * 16 * order**2, transcendentals=0),
    )(tables[0], tables[1], tables[3], source)


def body(rho, hamiltonian, couplings, bath_coef, damping, match_edges, left_rows, left_count):
    colours, pairs = match_edges.shape[1:3]
    early, late = exchanges(lax.axis_size("tier"), colours)
    me = lax.axis_index("tier").astype(jnp.int32)[None]
    left_fields = jnp.transpose(left_rows, (2, 1, 0))
    left_root = jnp.sqrt(left_fields[4].astype(F32))
    match_root = jnp.sqrt(match_edges[0, :, :, 4].astype(F32))
    tables = (me, left_fields, left_count, match_edges, left_root, match_root, bath_coef.T)

    plan = early + late

    def gather(sends, acc, scale, packs):
        arrived = [e.permute(s) for e, s in zip(plan, sends)]
        cut = len(early)
        acc = rows_call(early, [], pairs, scale, tables, couplings, arrived[:cut], acc)[0]
        acc, *sends = rows_call(late, packs, pairs, scale, tables, couplings, arrived[cut:], acc)
        return acc, sends

    sends = pack_call(early, pairs, tables, rho) + pack_call(late, pairs, tables, rho)
    first, sends = gather(sends, local_call(damping, hamiltonian, rho), 1.0, early)
    sends += pack_call(late, pairs, tables, first)
    return gather(sends, local_call(damping, hamiltonian, first, rho), 0.5 * STEP * STEP, [])[0]


def solution(mesh):
    placed = (
        P(("groups", "tier"), None, None, None),
        P(),
        P(),
        P("groups", None),
        P(("groups", "tier")),
        P("tier", None, None, None),
        P(),
        P(),
    )
    return jax.shard_map(
        body,
        mesh=mesh,
        in_specs=placed,
        out_specs=P(("groups", "tier"), None, None, None),
        check_vma=False,
    )
```

```python
import functools

import jax
import jax.numpy as jnp
from jax import lax
from jax.experimental import pallas as pl
from jax.experimental.pallas import tpu as pltpu
from jax.sharding import PartitionSpec as P

REACH = 4
STEP = 0.1
F32, BF16 = jnp.float32, jnp.bfloat16
SMEM = pl.BlockSpec(memory_space=pltpu.SMEM)
HBM = pl.BlockSpec(memory_space=pltpu.HBM)
ANY = pl.BlockSpec(memory_space=pl.ANY)
GRANT, LARGE_GRANT = 24 * 1024 * 1024, 56 * 1024 * 1024


class Exchange:
    def __init__(self, kind, step, size, colour=None, listed=True):
        self.kind, self.step, self.size, self.colour, self.listed = kind, step, size, colour, listed

    def peer(self, index, outgoing):
        size, step = self.size, self.step
        if self.kind == "swap":
            return index ^ step
        if self.kind == "other":
            lower = (index & step) == 0
            if isinstance(index, int):
                return (index + (-step if lower else step)) % size
            return lax.rem(index + jnp.where(lower, size - step, step), size)
        move = step if outgoing else size - step
        if isinstance(index, int):
            return (index + move) % size
        return lax.rem(index + move, size)

    def permute(self, value):
        return lax.ppermute(value, "tier", [(i, self.peer(i, True)) for i in range(self.size)])


def exchanges(size, colours):
    shifts, others, swaps, far, last = [], [], [], [], []
    for distance in range(1, REACH + 1):
        colour = distance.bit_length() - 1
        if distance != 1 << colour or colour >= colours:
            shifts += [Exchange("shift", distance, size), Exchange("shift", size - distance, size)]
            continue
        pair = [Exchange("swap", distance, size, colour), Exchange("other", distance, size)]
        if distance == REACH:
            last = pair
        else:
            swaps.append(pair[0])
            others.insert(0, pair[1])
    for colour in range(colours):
        if 1 << colour > REACH:
            far.append(Exchange("swap", 1 << colour, size, colour, listed=False))
    return shifts, others + swaps[:1], far + swaps[1:], last


def payload(exchange, pairs):
    return (pairs if exchange.colour is not None else 0) + (1 if exchange.listed else 0)


def when(condition, action):
    if condition is None:
        action()
    else:
        pl.when(condition)(action)


def split(value):
    high = value.astype(BF16)
    return high, (value - high.astype(F32)).astype(BF16)


def product(left, right):
    dot = functools.partial(jnp.dot, preferred_element_type=F32)
    return dot(left[0], right[0]) + (dot(left[0], right[1]) + dot(left[1], right[0]))


def outgoing_slots(exchange, me, mats, left_ref, match_ref):
    slots = []
    if exchange.colour is not None:
        for j in range(match_ref.shape[2]):
            slots.append(match_ref[0, exchange.colour, j, 0])
    if exchange.listed:
        peer = exchange.peer(me, True)
        slot = jnp.int32(0)
        for j in reversed(range(left_ref.shape[1])):
            source = left_ref[1, j, peer]
            slot = jnp.where(lax.div(source, mats) == me, lax.rem(source, mats), slot)
        slots.append(slot)
    return slots


def incoming_rows(exchange, me, mats, left_ref, count_ref, match_ref, left_root, match_root, bath_ref):
    rows = []

    def row(live, target, mode, flag, root):
        lower = flag == 1
        a = jnp.where(lower, jnp.float32(1), bath_ref[0, mode])
        b = jnp.where(lower, jnp.float32(0), bath_ref[1, mode])
        rows.append((live, target, mode, a * root, b * root))

    if exchange.colour is not None:
        c = exchange.colour
        for j in range(match_ref.shape[2]):
            row(None, match_ref[0, c, j, 0], match_ref[0, c, j, 2], match_ref[0, c, j, 3], match_root[c, j])
    if exchange.listed:
        peer = exchange.peer(me, False)
        found = [jnp.int32(0)] * 4 + [jnp.float32(0)]
        for j in range(left_ref.shape[1]):
            hit = (j < count_ref[me]) & (lax.div(left_ref[1, j, me], mats) == peer)
            here = [1, left_ref[0, j, me], left_ref[2, j, me], left_ref[3, j, me], left_root[j, me]]
            found = [jnp.where(hit, new, old) for new, old in zip(here, found)]
        row(found[0] == 1, found[1], found[2], found[3], found[4])
    return rows


def tables_kernel(plan, mats, me_ref, left_ref, count_ref, match_ref, left_root, match_root, bath_ref, whole, real):
    at = 0
    for exchange in plan:
        me = me_ref[0]
        slots = outgoing_slots(exchange, me, mats, left_ref, match_ref)
        rows = incoming_rows(exchange, me, mats, left_ref, count_ref, match_ref, left_root, match_root, bath_ref)
        for slot, (live, target, mode, a, b) in zip(slots, rows):
            whole[at, 0] = jnp.int32(1) if live is None else live.astype(jnp.int32)
            whole[at, 1], whole[at, 2], whole[at, 3] = target, mode, slot
            real[at, 0], real[at, 1] = a, b
            at += 1


def tables_call(plan, pairs, mats, tables):
    count = sum(payload(e, pairs) for e in plan)
    return pl.pallas_call(
        functools.partial(tables_kernel, plan, mats),
        in_specs=[SMEM] * 7,
        out_specs=[SMEM] * 2,
        out_shape=[jax.ShapeDtypeStruct((count, 4), jnp.int32), jax.ShapeDtypeStruct((count, 2), F32)],
        compiler_params=pltpu.CompilerParams(vmem_limit_bytes=GRANT),
    )(*tables)


def copy_slots(slots, source, sends, held, load_sems, sems):
    loads, stores = [], []
    for at, (slot, (send, place)) in enumerate(zip(slots, sends)):
        loads.append(pltpu.make_async_copy(source.at[slot], held.at[at], load_sems.at[at]))
        stores.append(pltpu.make_async_copy(held.at[at], send.at[place], sems.at[at]))
    for load in loads:
        load.start()
    for load, store in zip(loads, stores):
        load.wait()
        store.start()
    for store in stores:
        store.wait()


def places(plan, pairs, sends):
    return [(send, place) for e, send in zip(plan, sends) for place in range(payload(e, pairs))]


def first_pack_kernel(plan, pairs, mats, me_ref, left_ref, match_ref, source, *rest):
    slots = []
    for exchange in plan:
        slots += outgoing_slots(exchange, me_ref[0], mats, left_ref, match_ref)
    copy_slots(slots, source, places(plan, pairs, rest[:-3]), *rest[-3:])


def next_pack_kernel(plan, pairs, offset, whole, source, *rest):
    sends = places(plan, pairs, rest[:-3])
    copy_slots([whole[offset + at, 3] for at in range(len(sends))], source, sends, *rest[-3:])


def pack_call(kernel, plan, pairs, grant, scalars, source):
    order = source.shape[-1]
    sent = sum(payload(e, pairs) for e in plan)
    return list(
        pl.pallas_call(
            kernel,
            in_specs=[SMEM] * len(scalars) + [HBM],
            out_specs=[HBM] * len(plan),
            out_shape=[jax.ShapeDtypeStruct((payload(e, pairs), 2, order, order), F32) for e in plan],
            scratch_shapes=[
                pltpu.VMEM((sent, 2, order, order), F32),
                pltpu.SemaphoreType.DMA((sent,)),
                pltpu.SemaphoreType.DMA((sent,)),
            ],
            compiler_params=pltpu.CompilerParams(vmem_limit_bytes=grant),
            cost_estimate=pl.CostEstimate(flops=0, bytes_accessed=sent * 16 * order**2, transcendentals=0),
        )(*scalars, source)
    )


def commutator(density, hamiltonian):
    parts = []
    for part in (density[0], density[1]):
        halves = split(part)
        parts.append(product(hamiltonian, halves) - product(halves, hamiltonian))
    return parts[1], -parts[0]


def local_kernel(second, damping_ref, hamiltonian_ref, density_ref, *refs):
    out_ref = refs[-1]
    decay = damping_ref[pl.program_id(0)]
    density = (density_ref[0, 0], density_ref[0, 1])
    turned = commutator(density, split(hamiltonian_ref[...]))
    for part in range(2):
        slope = turned[part] - decay * density[part]
        if second:
            slope = refs[0][0, part] + STEP * density[part] + (0.5 * STEP * STEP) * slope
        out_ref[0, part] = slope


def local_call(damping, hamiltonian, *densities):
    mats, _, order, _ = densities[0].shape
    block = pl.BlockSpec((1, 2, order, order), lambda n: (n, 0, 0, 0))
    return pl.pallas_call(
        functools.partial(local_kernel, len(densities) == 2),
        grid=(mats,),
        in_specs=[SMEM, pl.BlockSpec((order, order), lambda n: (0, 0))] + [block] * len(densities),
        out_specs=block,
        out_shape=jax.ShapeDtypeStruct(densities[0].shape, F32),
        compiler_params=pltpu.CompilerParams(vmem_limit_bytes=GRANT),
        cost_estimate=pl.CostEstimate(
            flops=mats * 24 * order**3, bytes_accessed=mats * (1 + len(densities)) * 8 * order**2, transcendentals=0
        ),
    )(damping, hamiltonian, *densities)


def rows_kernel(plan, packs, pairs, offset, scale, whole, real, couplings_ref, *refs):
    arrivals = refs[: len(plan)]
    acc_in = refs[len(plan)]
    rest = refs[len(plan) + 1 :]
    acc_out, sends = rest[0], rest[1 : 1 + len(packs)]
    acc, landed, chosen, acc_sems, land_sems, mode_sems, send_sems = rest[1 + len(packs) :]
    mats = acc.shape[0]
    rows, lands, modes = [], [], []
    for exchange, arrival in zip(plan, arrivals):
        for place in range(payload(exchange, pairs)):
            at = len(rows)
            index = offset + at
            live = whole[index, 0] == 1 if exchange.listed and place == payload(exchange, pairs) - 1 else None
            row = (live, whole[index, 1], whole[index, 2], real[index, 0], real[index, 1])
            lands.append(pltpu.make_async_copy(arrival.at[place], landed.at[at], land_sems.at[at]))
            modes.append(pltpu.make_async_copy(couplings_ref.at[row[2]], chosen.at[at], mode_sems.at[at]))
            rows.append(row)
    for (live, *_), land, mode in zip(rows, lands, modes):
        when(live, land.start)
        when(live, mode.start)

    def touches(n):
        return functools.reduce(
            jnp.logical_or, [row[1] == n if row[0] is None else row[0] & (row[1] == n) for row in rows]
        )

    touched = [touches(n) for n in range(mats)]
    loads = [pltpu.make_async_copy(acc_in.at[n], acc.at[n], acc_sems.at[n]) for n in range(mats)]
    stores = [pltpu.make_async_copy(acc.at[n], acc_out.at[n], acc_sems.at[n]) for n in range(mats)]
    for n in range(mats):
        when(None if packs else touched[n], loads[n].start)

    def loaded():
        for n in range(mats):
            when(None if packs else touched[n], loads[n].wait)
        for untouched, copy in early:
            when(untouched, copy.start)

    early, late, copies = [], [], []
    for at, (send, place) in enumerate(places(packs, pairs, sends)):
        slot = whole[at, 3]
        copy = pltpu.make_async_copy(acc.at[slot], send.at[place], send_sems.at[at])
        busy = touches(slot)
        copies.append(copy)
        late.append((busy, copy))
        early.append((jnp.logical_not(busy), copy))
    if rows[0][0] is not None:
        loaded()
    for at, (live, target, _, a, b) in enumerate(rows):

        def add(at=at, target=target, a=a, b=b, first=at == 0 and live is None):
            modes[at].wait()
            lands[at].wait()
            coupling = split(chosen[at])
            real, imag = split(landed[at, 0]), split(landed[at, 1])
            left_re, right_re = product(coupling, real), product(real, coupling)
            left_im, right_im = product(coupling, imag), product(imag, coupling)
            edge_re = a * (left_re - right_re) - b * (left_im + right_im)
            edge_im = a * (left_im - right_im) + b * (left_re + right_re)
            if first:
                loaded()
            acc[target, 0] += scale * edge_im
            acc[target, 1] -= scale * edge_re

        when(live, add)
    for busy, copy in late:
        when(busy, copy.start)
    for n in range(mats):
        when(touched[n], stores[n].start)
    for copy in copies:
        copy.wait()
    for n in range(mats):
        when(touched[n], stores[n].wait)


def rows_call(plan, packs, pairs, offset, scale, scalars, couplings, arrivals, acc):
    mats, _, order, _ = acc.shape
    count = sum(payload(e, pairs) for e in plan)
    sent = sum(payload(e, pairs) for e in packs)
    shapes = [jax.ShapeDtypeStruct(acc.shape, F32)]
    shapes += [jax.ShapeDtypeStruct((payload(e, pairs), 2, order, order), F32) for e in packs]
    return pl.pallas_call(
        functools.partial(rows_kernel, plan, packs, pairs, offset, scale),
        in_specs=[SMEM] * 2 + [HBM] + [ANY] * len(plan) + [HBM],
        out_specs=[HBM] * len(shapes),
        out_shape=shapes,
        input_output_aliases={3 + len(plan): 0},
        scratch_shapes=[
            pltpu.VMEM((mats, 2, order, order), F32),
            pltpu.VMEM((count, 2, order, order), F32),
            pltpu.VMEM((count, order, order), F32),
            pltpu.SemaphoreType.DMA((mats,)),
            pltpu.SemaphoreType.DMA((count,)),
            pltpu.SemaphoreType.DMA((count,)),
            pltpu.SemaphoreType.DMA((max(sent, 1),)),
        ],
        compiler_params=pltpu.CompilerParams(vmem_limit_bytes=GRANT),
        cost_estimate=pl.CostEstimate(flops=0, bytes_accessed=0, transcendentals=0),
    )(*scalars, couplings, *arrivals, acc)


def body(rho, hamiltonian, couplings, bath_coef, damping, match_edges, left_rows, left_count):
    colours, pairs = match_edges.shape[1:3]
    shifts, early, middle, last = exchanges(lax.axis_size("tier"), colours)
    plan = shifts + early + middle + last
    mats = rho.shape[0]
    me = lax.axis_index("tier").astype(jnp.int32)[None]
    left_fields = jnp.transpose(left_rows, (2, 1, 0))
    left_root = jnp.sqrt(left_fields[4].astype(F32))
    match_root = jnp.sqrt(match_edges[0, :, :, 4].astype(F32))
    tables = (me, left_fields, left_count, match_edges, left_root, match_root, bath_coef.T)

    first_tables = (tables[0], tables[1], tables[3])
    scalars = tables_call(plan, pairs, mats, tables)

    def size(group):
        return sum(payload(e, pairs) for e in group)

    def gather(sends, acc, scale, packs, groups):
        arrived = [e.permute(s) for e, s in zip(plan, sends)]
        at, offset = 0, 0
        for group in groups:
            sent = packs if group is groups[-1] else []
            got = arrived[at : at + len(group)]
            acc, *out = rows_call(group, sent, pairs, offset, scale, scalars, couplings, got, acc)
            at, offset = at + len(group), offset + size(group)
        return acc, out

    rest = plan[len(shifts) :]
    pack = functools.partial(first_pack_kernel, shifts, pairs, mats)
    sends = pack_call(pack, shifts, pairs, LARGE_GRANT, first_tables, rho)
    pack = functools.partial(first_pack_kernel, rest, pairs, mats)
    sends += pack_call(pack, rest, pairs, GRANT, first_tables, rho)
    groups = [group for group in (shifts + early, middle, last) if group]
    first, sends = gather(sends, local_call(damping, hamiltonian, rho), 1.0, shifts, groups)

    pack = functools.partial(next_pack_kernel, rest, pairs, size(shifts))
    sends += pack_call(pack, rest, pairs, GRANT, scalars[:1], first)
    groups = [group for group in (shifts + early, middle + last) if group]
    return gather(sends, local_call(damping, hamiltonian, first, rho), 0.5 * STEP * STEP, [], groups)[0]


def solution(mesh):
    placed = (
        P(("groups", "tier"), None, None, None),
        P(),
        P(),
        P("groups", None),
        P(("groups", "tier")),
        P("tier", None, None, None),
        P(),
        P(),
    )
    return jax.shard_map(
        body,
        mesh=mesh,
        in_specs=placed,
        out_specs=P(("groups", "tier"), None, None, None),
        check_vma=False,
    )
```

```python
import functools

import jax
import jax.numpy as jnp
from jax import lax
from jax.experimental import pallas as pl
from jax.experimental.pallas import tpu as pltpu
from jax.sharding import PartitionSpec as P

REACH = 4
STEP = 0.1
F32, BF16 = jnp.float32, jnp.bfloat16
SMEM = pl.BlockSpec(memory_space=pltpu.SMEM)
HBM = pl.BlockSpec(memory_space=pltpu.HBM)
ANY = pl.BlockSpec(memory_space=pl.ANY)
GRANT, LARGE_GRANT = 24 * 1024 * 1024, 56 * 1024 * 1024


class Exchange:
    def __init__(self, kind, step, size, colour=None, listed=True):
        self.kind, self.step, self.size, self.colour, self.listed = kind, step, size, colour, listed

    def peer(self, index, outgoing):
        size, step = self.size, self.step
        if self.kind == "swap":
            return index ^ step
        if self.kind == "other":
            lower = (index & step) == 0
            if isinstance(index, int):
                return (index + (-step if lower else step)) % size
            return lax.rem(index + jnp.where(lower, size - step, step), size)
        move = step if outgoing else size - step
        if isinstance(index, int):
            return (index + move) % size
        return lax.rem(index + move, size)

    def permute(self, value):
        return lax.ppermute(value, "tier", [(i, self.peer(i, True)) for i in range(self.size)])


def exchanges(size, colours):
    shifts, others, swaps, far, last = [], [], [], [], []
    for distance in range(1, REACH + 1):
        colour = distance.bit_length() - 1
        if distance != 1 << colour or colour >= colours:
            shifts += [Exchange("shift", distance, size), Exchange("shift", size - distance, size)]
            continue
        pair = [Exchange("swap", distance, size, colour), Exchange("other", distance, size)]
        if distance == REACH:
            last = pair
        else:
            swaps.append(pair[0])
            others.insert(0, pair[1])
    for colour in range(colours):
        if 1 << colour > REACH:
            far.append(Exchange("swap", 1 << colour, size, colour, listed=False))
    return shifts, others + swaps[:1], far + swaps[1:], last


def payload(exchange, pairs):
    return (pairs if exchange.colour is not None else 0) + (1 if exchange.listed else 0)


def when(condition, action):
    if condition is None:
        action()
    else:
        pl.when(condition)(action)


def split(value):
    high = value.astype(BF16)
    return high, (value - high.astype(F32)).astype(BF16)


def product(left, right):
    dot = functools.partial(jnp.dot, preferred_element_type=F32)
    return dot(left[0], right[0]) + (dot(left[0], right[1]) + dot(left[1], right[0]))


def outgoing_slots(exchange, me, mats, left_ref, match_ref):
    slots = []
    if exchange.colour is not None:
        for j in range(match_ref.shape[2]):
            slots.append(match_ref[0, exchange.colour, j, 0])
    if exchange.listed:
        peer = exchange.peer(me, True)
        slot = jnp.int32(0)
        for j in reversed(range(left_ref.shape[1])):
            source = left_ref[1, j, peer]
            slot = jnp.where(lax.div(source, mats) == me, lax.rem(source, mats), slot)
        slots.append(slot)
    return slots


def incoming_rows(exchange, me, mats, left_ref, count_ref, match_ref, left_root, match_root, bath_ref):
    rows = []

    def row(live, target, mode, flag, root):
        lower = flag == 1
        a = jnp.where(lower, jnp.float32(1), bath_ref[0, mode])
        b = jnp.where(lower, jnp.float32(0), bath_ref[1, mode])
        rows.append((live, target, mode, a * root, b * root))

    if exchange.colour is not None:
        c = exchange.colour
        for j in range(match_ref.shape[2]):
            row(None, match_ref[0, c, j, 0], match_ref[0, c, j, 2], match_ref[0, c, j, 3], match_root[c, j])
    if exchange.listed:
        peer = exchange.peer(me, False)
        found = [jnp.int32(0)] * 4 + [jnp.float32(0)]
        for j in range(left_ref.shape[1]):
            hit = (j < count_ref[me]) & (lax.div(left_ref[1, j, me], mats) == peer)
            here = [1, left_ref[0, j, me], left_ref[2, j, me], left_ref[3, j, me], left_root[j, me]]
            found = [jnp.where(hit, new, old) for new, old in zip(here, found)]
        row(found[0] == 1, found[1], found[2], found[3], found[4])
    return rows


def tables_kernel(plan, mats, me_ref, left_ref, count_ref, match_ref, left_root, match_root, bath_ref, whole, real):
    at = 0
    for exchange in plan:
        me = me_ref[0]
        slots = outgoing_slots(exchange, me, mats, left_ref, match_ref)
        rows = incoming_rows(exchange, me, mats, left_ref, count_ref, match_ref, left_root, match_root, bath_ref)
        for slot, (live, target, mode, a, b) in zip(slots, rows):
            whole[at, 0] = jnp.int32(1) if live is None else live.astype(jnp.int32)
            whole[at, 1], whole[at, 2], whole[at, 3] = target, mode, slot
            real[at, 0], real[at, 1] = a, b
            at += 1


def tables_call(plan, pairs, mats, tables):
    count = sum(payload(e, pairs) for e in plan)
    return pl.pallas_call(
        functools.partial(tables_kernel, plan, mats),
        in_specs=[SMEM] * 7,
        out_specs=[SMEM] * 2,
        out_shape=[jax.ShapeDtypeStruct((count, 4), jnp.int32), jax.ShapeDtypeStruct((count, 2), F32)],
        compiler_params=pltpu.CompilerParams(vmem_limit_bytes=GRANT),
    )(*tables)


def copy_slots(slots, source, sends, sems, load_sems=None, held=None):
    loads, stores = [], []
    for at, (slot, (send, place)) in enumerate(zip(slots, sends)):
        if held is None:
            stores.append(pltpu.make_async_copy(source.at[slot], send.at[place], sems.at[at]))
            continue
        loads.append(pltpu.make_async_copy(source.at[slot], held.at[at], load_sems.at[at]))
        stores.append(pltpu.make_async_copy(held.at[at], send.at[place], sems.at[at]))
    for load in loads:
        load.start()
    for at, store in enumerate(stores):
        if loads:
            loads[at].wait()
        store.start()
    for store in stores:
        store.wait()


def places(plan, pairs, sends):
    return [(send, place) for e, send in zip(plan, sends) for place in range(payload(e, pairs))]


def first_pack_kernel(plan, pairs, mats, me_ref, left_ref, match_ref, source, *rest):
    slots = []
    for exchange in plan:
        slots += outgoing_slots(exchange, me_ref[0], mats, left_ref, match_ref)
    copy_slots(slots, source, places(plan, pairs, rest[: len(plan)]), *rest[len(plan) :])


def next_pack_kernel(plan, pairs, offset, whole, source, *rest):
    sends = places(plan, pairs, rest[: len(plan)])
    copy_slots([whole[offset + at, 3] for at in range(len(sends))], source, sends, *rest[len(plan) :])


def pack_call(kernel, plan, pairs, grant, scalars, source, in_vmem=False):
    order = source.shape[-1]
    sent = sum(payload(e, pairs) for e in plan)
    buffer = pltpu.VMEM if in_vmem else jax.ShapeDtypeStruct
    scratch = [pltpu.SemaphoreType.DMA((sent,))]
    if not in_vmem:
        scratch += [pltpu.SemaphoreType.DMA((sent,)), pltpu.VMEM((sent, 2, order, order), F32)]
    return list(
        pl.pallas_call(
            kernel,
            in_specs=[SMEM] * len(scalars) + [HBM],
            out_specs=[pl.BlockSpec(memory_space=pltpu.VMEM) if in_vmem else HBM] * len(plan),
            out_shape=[buffer((payload(e, pairs), 2, order, order), F32) for e in plan],
            scratch_shapes=scratch,
            compiler_params=pltpu.CompilerParams(vmem_limit_bytes=grant),
            cost_estimate=pl.CostEstimate(flops=0, bytes_accessed=sent * 16 * order**2, transcendentals=0),
        )(*scalars, source)
    )


def commutator(density, hamiltonian):
    parts = []
    for part in (density[0], density[1]):
        halves = split(part)
        parts.append(product(hamiltonian, halves) - product(halves, hamiltonian))
    return parts[1], -parts[0]


def local_kernel(second, damping_ref, hamiltonian_ref, density_ref, *refs):
    out_ref = refs[-1]
    decay = damping_ref[pl.program_id(0)]
    density = (density_ref[0, 0], density_ref[0, 1])
    turned = commutator(density, split(hamiltonian_ref[...]))
    for part in range(2):
        slope = turned[part] - decay * density[part]
        if second:
            slope = refs[0][0, part] + STEP * density[part] + (0.5 * STEP * STEP) * slope
        out_ref[0, part] = slope


def local_call(damping, hamiltonian, *densities):
    mats, _, order, _ = densities[0].shape
    block = pl.BlockSpec((1, 2, order, order), lambda n: (n, 0, 0, 0))
    return pl.pallas_call(
        functools.partial(local_kernel, len(densities) == 2),
        grid=(mats,),
        in_specs=[SMEM, pl.BlockSpec((order, order), lambda n: (0, 0))] + [block] * len(densities),
        out_specs=block,
        out_shape=jax.ShapeDtypeStruct(densities[0].shape, F32),
        compiler_params=pltpu.CompilerParams(vmem_limit_bytes=GRANT),
        cost_estimate=pl.CostEstimate(
            flops=mats * 24 * order**3, bytes_accessed=mats * (1 + len(densities)) * 8 * order**2, transcendentals=0
        ),
    )(damping, hamiltonian, *densities)


def rows_kernel(plan, packs, pairs, offset, scale, whole, real, couplings_ref, *refs):
    arrivals = refs[: len(plan)]
    acc_in = refs[len(plan)]
    rest = refs[len(plan) + 1 :]
    acc_out, sends = rest[0], rest[1 : 1 + len(packs)]
    acc, landed, chosen, acc_sems, land_sems, mode_sems, send_sems = rest[1 + len(packs) :]
    mats = acc.shape[0]
    rows, lands, modes = [], [], []
    for exchange, arrival in zip(plan, arrivals):
        for place in range(payload(exchange, pairs)):
            at = len(rows)
            index = offset + at
            live = whole[index, 0] == 1 if exchange.listed and place == payload(exchange, pairs) - 1 else None
            row = (live, whole[index, 1], whole[index, 2], real[index, 0], real[index, 1])
            lands.append(pltpu.make_async_copy(arrival.at[place], landed.at[at], land_sems.at[at]))
            modes.append(pltpu.make_async_copy(couplings_ref.at[row[2]], chosen.at[at], mode_sems.at[at]))
            rows.append(row)
    for (live, *_), land, mode in zip(rows, lands, modes):
        when(live, land.start)
        when(live, mode.start)

    def touches(n):
        return functools.reduce(
            jnp.logical_or, [row[1] == n if row[0] is None else row[0] & (row[1] == n) for row in rows]
        )

    touched = [touches(n) for n in range(mats)]
    loads = [pltpu.make_async_copy(acc_in.at[n], acc.at[n], acc_sems.at[n]) for n in range(mats)]
    stores = [pltpu.make_async_copy(acc.at[n], acc_out.at[n], acc_sems.at[n]) for n in range(mats)]
    for n in range(mats):
        when(None if packs else touched[n], loads[n].start)

    def loaded():
        for n in range(mats):
            when(None if packs else touched[n], loads[n].wait)
        for untouched, copy in early:
            when(untouched, copy.start)

    early, late, copies = [], [], []
    for at, (send, place) in enumerate(places(packs, pairs, sends)):
        slot = whole[at, 3]
        copy = pltpu.make_async_copy(acc.at[slot], send.at[place], send_sems.at[at])
        busy = touches(slot)
        copies.append(copy)
        late.append((busy, copy))
        early.append((jnp.logical_not(busy), copy))
    if rows[0][0] is not None:
        loaded()
    for at, (live, target, _, a, b) in enumerate(rows):

        def add(at=at, target=target, a=a, b=b, first=at == 0 and live is None):
            modes[at].wait()
            lands[at].wait()
            coupling = split(chosen[at])
            real, imag = split(landed[at, 0]), split(landed[at, 1])
            left_re, right_re = product(coupling, real), product(real, coupling)
            left_im, right_im = product(coupling, imag), product(imag, coupling)
            edge_re = a * (left_re - right_re) - b * (left_im + right_im)
            edge_im = a * (left_im - right_im) + b * (left_re + right_re)
            if first:
                loaded()
            acc[target, 0] += scale * edge_im
            acc[target, 1] -= scale * edge_re

        when(live, add)
    for busy, copy in late:
        when(busy, copy.start)
    for n in range(mats):
        when(touched[n], stores[n].start)
    for copy in copies:
        copy.wait()
    for n in range(mats):
        when(touched[n], stores[n].wait)


def rows_call(plan, packs, pairs, offset, scale, scalars, couplings, arrivals, acc):
    mats, _, order, _ = acc.shape
    count = sum(payload(e, pairs) for e in plan)
    sent = sum(payload(e, pairs) for e in packs)
    shapes = [jax.ShapeDtypeStruct(acc.shape, F32)]
    shapes += [jax.ShapeDtypeStruct((payload(e, pairs), 2, order, order), F32) for e in packs]
    return pl.pallas_call(
        functools.partial(rows_kernel, plan, packs, pairs, offset, scale),
        in_specs=[SMEM] * 2 + [HBM] + [ANY] * len(plan) + [HBM],
        out_specs=[HBM] * len(shapes),
        out_shape=shapes,
        input_output_aliases={3 + len(plan): 0},
        scratch_shapes=[
            pltpu.VMEM((mats, 2, order, order), F32),
            pltpu.VMEM((count, 2, order, order), F32),
            pltpu.VMEM((count, order, order), F32),
            pltpu.SemaphoreType.DMA((mats,)),
            pltpu.SemaphoreType.DMA((count,)),
            pltpu.SemaphoreType.DMA((count,)),
            pltpu.SemaphoreType.DMA((max(sent, 1),)),
        ],
        compiler_params=pltpu.CompilerParams(vmem_limit_bytes=GRANT),
        cost_estimate=pl.CostEstimate(flops=0, bytes_accessed=0, transcendentals=0),
    )(*scalars, couplings, *arrivals, acc)


def body(rho, hamiltonian, couplings, bath_coef, damping, match_edges, left_rows, left_count):
    colours, pairs = match_edges.shape[1:3]
    shifts, early, middle, last = exchanges(lax.axis_size("tier"), colours)
    plan = shifts + early + middle + last
    mats = rho.shape[0]
    me = lax.axis_index("tier").astype(jnp.int32)[None]
    left_fields = jnp.transpose(left_rows, (2, 1, 0))
    left_root = jnp.sqrt(left_fields[4].astype(F32))
    match_root = jnp.sqrt(match_edges[0, :, :, 4].astype(F32))
    tables = (me, left_fields, left_count, match_edges, left_root, match_root, bath_coef.T)

    first_tables = (tables[0], tables[1], tables[3])
    scalars = tables_call(plan, pairs, mats, tables)

    def size(group):
        return sum(payload(e, pairs) for e in group)

    def gather(sends, acc, scale, packs, groups):
        arrived = [e.permute(s) for e, s in zip(plan, sends)]
        at, offset = 0, 0
        for group in groups:
            sent = packs if group is groups[-1] else []
            got = arrived[at : at + len(group)]
            acc, *out = rows_call(group, sent, pairs, offset, scale, scalars, couplings, got, acc)
            at, offset = at + len(group), offset + size(group)
        return acc, out

    rest = plan[len(shifts) :]
    pack = functools.partial(first_pack_kernel, shifts, pairs, mats)
    sends = pack_call(pack, shifts, pairs, LARGE_GRANT, first_tables, rho, in_vmem=True)
    pack = functools.partial(first_pack_kernel, rest, pairs, mats)
    sends += pack_call(pack, rest, pairs, GRANT, first_tables, rho)
    groups = [group for group in (shifts + early, middle, last) if group]
    first, sends = gather(sends, local_call(damping, hamiltonian, rho), 1.0, shifts, groups)

    pack = functools.partial(next_pack_kernel, rest, pairs, size(shifts))
    sends += pack_call(pack, rest, pairs, GRANT, scalars[:1], first)
    groups = [group for group in (shifts + early, middle[:1], middle[1:] + last) if group]
    return gather(sends, local_call(damping, hamiltonian, first, rho), 0.5 * STEP * STEP, [], groups)[0]


def solution(mesh):
    placed = (
        P(("groups", "tier"), None, None, None),
        P(),
        P(),
        P("groups", None),
        P(("groups", "tier")),
        P("tier", None, None, None),
        P(),
        P(),
    )
    return jax.shard_map(
        body,
        mesh=mesh,
        in_specs=placed,
        out_specs=P(("groups", "tier"), None, None, None),
        check_vma=False,
    )
```

```python
import functools

import jax
import jax.numpy as jnp
from jax import lax
from jax.experimental import pallas as pl
from jax.experimental.pallas import tpu as pltpu
from jax.sharding import PartitionSpec as P

REACH = 4
STEP = 0.1
F32, BF16 = jnp.float32, jnp.bfloat16
SMEM = pl.BlockSpec(memory_space=pltpu.SMEM)
HBM = pl.BlockSpec(memory_space=pltpu.HBM)
ANY = pl.BlockSpec(memory_space=pl.ANY)
GRANT, LARGE_GRANT = 24 * 1024 * 1024, 56 * 1024 * 1024


class Exchange:
    def __init__(self, kind, step, size, colour=None, listed=True):
        self.kind, self.step, self.size, self.colour, self.listed = kind, step, size, colour, listed

    def peer(self, index, outgoing):
        size, step = self.size, self.step
        if self.kind == "swap":
            return index ^ step
        if self.kind == "other":
            lower = (index & step) == 0
            if isinstance(index, int):
                return (index + (-step if lower else step)) % size
            return lax.rem(index + jnp.where(lower, size - step, step), size)
        move = step if outgoing else size - step
        if isinstance(index, int):
            return (index + move) % size
        return lax.rem(index + move, size)

    def permute(self, value):
        return lax.ppermute(value, "tier", [(i, self.peer(i, True)) for i in range(self.size)])


def exchanges(size, colours):
    shifts, short, swaps, far, others = [], [], [], [], []
    for distance in range(1, REACH + 1):
        colour = distance.bit_length() - 1
        if distance != 1 << colour or colour >= colours:
            shifts += [Exchange("shift", distance, size), Exchange("shift", size - distance, size)]
            continue
        swaps.append(Exchange("swap", distance, size, colour))
        other = Exchange("other", distance, size)
        if distance == REACH:
            others.append(other)
        else:
            short.insert(0, other)
    for colour in range(colours):
        if 1 << colour > REACH:
            far.append(Exchange("swap", 1 << colour, size, colour, listed=False))
    return shifts, short + swaps[:1], far, swaps[1:], others


def payload(exchange, pairs):
    return (pairs if exchange.colour is not None else 0) + (1 if exchange.listed else 0)


def when(condition, action):
    if condition is None:
        action()
    else:
        pl.when(condition)(action)


def split(value):
    high = value.astype(BF16)
    return high, (value - high.astype(F32)).astype(BF16)


def product(left, right):
    dot = functools.partial(jnp.dot, preferred_element_type=F32)
    return dot(left[0], right[0]) + (dot(left[0], right[1]) + dot(left[1], right[0]))


def outgoing_slots(exchange, me, mats, left_ref, match_ref):
    slots = []
    if exchange.colour is not None:
        for j in range(match_ref.shape[2]):
            slots.append(match_ref[0, exchange.colour, j, 0])
    if exchange.listed:
        peer = exchange.peer(me, True)
        slot = jnp.int32(0)
        for j in reversed(range(left_ref.shape[1])):
            source = left_ref[1, j, peer]
            slot = jnp.where(lax.div(source, mats) == me, lax.rem(source, mats), slot)
        slots.append(slot)
    return slots


def incoming_rows(exchange, me, mats, left_ref, count_ref, match_ref, left_root, match_root, bath_ref):
    rows = []

    def row(live, target, mode, flag, root):
        lower = flag == 1
        a = jnp.where(lower, jnp.float32(1), bath_ref[0, mode])
        b = jnp.where(lower, jnp.float32(0), bath_ref[1, mode])
        rows.append((live, target, mode, a * root, b * root))

    if exchange.colour is not None:
        c = exchange.colour
        for j in range(match_ref.shape[2]):
            row(None, match_ref[0, c, j, 0], match_ref[0, c, j, 2], match_ref[0, c, j, 3], match_root[c, j])
    if exchange.listed:
        peer = exchange.peer(me, False)
        found = [jnp.int32(0)] * 4 + [jnp.float32(0)]
        for j in range(left_ref.shape[1]):
            hit = (j < count_ref[me]) & (lax.div(left_ref[1, j, me], mats) == peer)
            here = [1, left_ref[0, j, me], left_ref[2, j, me], left_ref[3, j, me], left_root[j, me]]
            found = [jnp.where(hit, new, old) for new, old in zip(here, found)]
        row(found[0] == 1, found[1], found[2], found[3], found[4])
    return rows


def tables_kernel(plan, mats, me_ref, left_ref, count_ref, match_ref, left_root, match_root, bath_ref, whole, real):
    at = 0
    for exchange in plan:
        me = me_ref[0]
        slots = outgoing_slots(exchange, me, mats, left_ref, match_ref)
        rows = incoming_rows(exchange, me, mats, left_ref, count_ref, match_ref, left_root, match_root, bath_ref)
        for slot, (live, target, mode, a, b) in zip(slots, rows):
            whole[at, 0] = jnp.int32(1) if live is None else live.astype(jnp.int32)
            whole[at, 1], whole[at, 2], whole[at, 3] = target, mode, slot
            real[at, 0], real[at, 1] = a, b
            at += 1


def tables_call(plan, pairs, mats, tables):
    count = sum(payload(e, pairs) for e in plan)
    return pl.pallas_call(
        functools.partial(tables_kernel, plan, mats),
        in_specs=[SMEM] * 7,
        out_specs=[SMEM] * 2,
        out_shape=[jax.ShapeDtypeStruct((count, 4), jnp.int32), jax.ShapeDtypeStruct((count, 2), F32)],
        compiler_params=pltpu.CompilerParams(vmem_limit_bytes=GRANT),
    )(*tables)


def copy_slots(slots, source, sends, sems, load_sems=None, held=None):
    loads, stores = [], []
    for at, (slot, (send, place)) in enumerate(zip(slots, sends)):
        if held is None:
            stores.append(pltpu.make_async_copy(source.at[slot], send.at[place], sems.at[at]))
            continue
        loads.append(pltpu.make_async_copy(source.at[slot], held.at[at], load_sems.at[at]))
        stores.append(pltpu.make_async_copy(held.at[at], send.at[place], sems.at[at]))
    for load in loads:
        load.start()
    for at, store in enumerate(stores):
        if loads:
            loads[at].wait()
        store.start()
    for store in stores:
        store.wait()


def places(plan, pairs, sends):
    return [(send, place) for e, send in zip(plan, sends) for place in range(payload(e, pairs))]


def first_pack_kernel(plan, pairs, mats, me_ref, left_ref, match_ref, source, *rest):
    slots = []
    for exchange in plan:
        slots += outgoing_slots(exchange, me_ref[0], mats, left_ref, match_ref)
    copy_slots(slots, source, places(plan, pairs, rest[: len(plan)]), *rest[len(plan) :])


def next_pack_kernel(plan, pairs, offset, whole, source, *rest):
    sends = places(plan, pairs, rest[: len(plan)])
    copy_slots([whole[offset + at, 3] for at in range(len(sends))], source, sends, *rest[len(plan) :])


def pack_call(kernel, plan, pairs, grant, scalars, source, in_vmem=False):
    order = source.shape[-1]
    sent = sum(payload(e, pairs) for e in plan)
    buffer = pltpu.VMEM if in_vmem else jax.ShapeDtypeStruct
    scratch = [pltpu.SemaphoreType.DMA((sent,))]
    if not in_vmem:
        scratch += [pltpu.SemaphoreType.DMA((sent,)), pltpu.VMEM((sent, 2, order, order), F32)]
    return list(
        pl.pallas_call(
            kernel,
            in_specs=[SMEM] * len(scalars) + [HBM],
            out_specs=[pl.BlockSpec(memory_space=pltpu.VMEM) if in_vmem else HBM] * len(plan),
            out_shape=[buffer((payload(e, pairs), 2, order, order), F32) for e in plan],
            scratch_shapes=scratch,
            compiler_params=pltpu.CompilerParams(vmem_limit_bytes=grant),
            cost_estimate=pl.CostEstimate(flops=0, bytes_accessed=sent * 16 * order**2, transcendentals=0),
        )(*scalars, source)
    )


def commutator(density, hamiltonian):
    parts = []
    for part in (density[0], density[1]):
        halves = split(part)
        parts.append(product(hamiltonian, halves) - product(halves, hamiltonian))
    return parts[1], -parts[0]


def local_kernel(second, damping_ref, hamiltonian_ref, density_ref, *refs):
    out_ref = refs[-1]
    decay = damping_ref[pl.program_id(0)]
    density = (density_ref[0, 0], density_ref[0, 1])
    turned = commutator(density, split(hamiltonian_ref[...]))
    for part in range(2):
        slope = turned[part] - decay * density[part]
        if second:
            slope = refs[0][0, part] + STEP * density[part] + (0.5 * STEP * STEP) * slope
        out_ref[0, part] = slope


def local_call(damping, hamiltonian, *densities):
    mats, _, order, _ = densities[0].shape
    block = pl.BlockSpec((1, 2, order, order), lambda n: (n, 0, 0, 0))
    return pl.pallas_call(
        functools.partial(local_kernel, len(densities) == 2),
        grid=(mats,),
        in_specs=[SMEM, pl.BlockSpec((order, order), lambda n: (0, 0))] + [block] * len(densities),
        out_specs=block,
        out_shape=jax.ShapeDtypeStruct(densities[0].shape, F32),
        compiler_params=pltpu.CompilerParams(vmem_limit_bytes=GRANT),
        cost_estimate=pl.CostEstimate(
            flops=mats * 24 * order**3, bytes_accessed=mats * (1 + len(densities)) * 8 * order**2, transcendentals=0
        ),
    )(damping, hamiltonian, *densities)


def rows_kernel(plan, packs, pairs, offsets, scale, whole, real, couplings_ref, *refs):
    arrivals = refs[: len(plan)]
    acc_in = refs[len(plan)]
    rest = refs[len(plan) + 1 :]
    acc_out, sends = rest[0], rest[1 : 1 + len(packs)]
    acc, landed, chosen, acc_sems, land_sems, mode_sems, send_sems = rest[1 + len(packs) :]
    mats = acc.shape[0]
    rows, lands, modes = [], [], []
    for exchange, offset, arrival in zip(plan, offsets, arrivals):
        for place in range(payload(exchange, pairs)):
            at = len(rows)
            index = offset + place
            live = whole[index, 0] == 1 if exchange.listed and place == payload(exchange, pairs) - 1 else None
            row = (live, whole[index, 1], whole[index, 2], real[index, 0], real[index, 1])
            lands.append(pltpu.make_async_copy(arrival.at[place], landed.at[at], land_sems.at[at]))
            modes.append(pltpu.make_async_copy(couplings_ref.at[row[2]], chosen.at[at], mode_sems.at[at]))
            rows.append(row)
    for (live, *_), land, mode in zip(rows, lands, modes):
        when(live, land.start)
        when(live, mode.start)

    def touches(n):
        return functools.reduce(
            jnp.logical_or, [row[1] == n if row[0] is None else row[0] & (row[1] == n) for row in rows]
        )

    touched = [touches(n) for n in range(mats)]
    loads = [pltpu.make_async_copy(acc_in.at[n], acc.at[n], acc_sems.at[n]) for n in range(mats)]
    stores = [pltpu.make_async_copy(acc.at[n], acc_out.at[n], acc_sems.at[n]) for n in range(mats)]
    for n in range(mats):
        when(None if packs else touched[n], loads[n].start)

    def loaded():
        for n in range(mats):
            when(None if packs else touched[n], loads[n].wait)
        for untouched, copy in early:
            when(untouched, copy.start)

    early, late, copies = [], [], []
    for at, (send, place) in enumerate(places(packs, pairs, sends)):
        slot = whole[at, 3]
        copy = pltpu.make_async_copy(acc.at[slot], send.at[place], send_sems.at[at])
        busy = touches(slot)
        copies.append(copy)
        late.append((busy, copy))
        early.append((jnp.logical_not(busy), copy))
    if rows[0][0] is not None:
        loaded()
    for at, (live, target, _, a, b) in enumerate(rows):

        def add(at=at, target=target, a=a, b=b, first=at == 0 and live is None):
            modes[at].wait()
            lands[at].wait()
            coupling = split(chosen[at])
            real, imag = split(landed[at, 0]), split(landed[at, 1])
            left_re, right_re = product(coupling, real), product(real, coupling)
            left_im, right_im = product(coupling, imag), product(imag, coupling)
            edge_re = a * (left_re - right_re) - b * (left_im + right_im)
            edge_im = a * (left_im - right_im) + b * (left_re + right_re)
            if first:
                loaded()
            acc[target, 0] += scale * edge_im
            acc[target, 1] -= scale * edge_re

        when(live, add)
    for busy, copy in late:
        when(busy, copy.start)
    for n in range(mats):
        when(touched[n], stores[n].start)
    for copy in copies:
        copy.wait()
    for n in range(mats):
        when(touched[n], stores[n].wait)


def rows_call(plan, packs, pairs, offsets, scale, scalars, couplings, arrivals, acc):
    mats, _, order, _ = acc.shape
    count = sum(payload(e, pairs) for e in plan)
    sent = sum(payload(e, pairs) for e in packs)
    shapes = [jax.ShapeDtypeStruct(acc.shape, F32)]
    shapes += [jax.ShapeDtypeStruct((payload(e, pairs), 2, order, order), F32) for e in packs]
    return pl.pallas_call(
        functools.partial(rows_kernel, plan, packs, pairs, offsets, scale),
        in_specs=[SMEM] * 2 + [HBM] + [ANY] * len(plan) + [HBM],
        out_specs=[HBM] * len(shapes),
        out_shape=shapes,
        input_output_aliases={3 + len(plan): 0},
        scratch_shapes=[
            pltpu.VMEM((mats, 2, order, order), F32),
            pltpu.VMEM((count, 2, order, order), F32),
            pltpu.VMEM((count, order, order), F32),
            pltpu.SemaphoreType.DMA((mats,)),
            pltpu.SemaphoreType.DMA((count,)),
            pltpu.SemaphoreType.DMA((count,)),
            pltpu.SemaphoreType.DMA((max(sent, 1),)),
        ],
        compiler_params=pltpu.CompilerParams(vmem_limit_bytes=GRANT),
        cost_estimate=pl.CostEstimate(flops=0, bytes_accessed=0, transcendentals=0),
    )(*scalars, couplings, *arrivals, acc)


def body(rho, hamiltonian, couplings, bath_coef, damping, match_edges, left_rows, left_count):
    colours, pairs = match_edges.shape[1:3]
    shifts, early, far, swaps, others = exchanges(lax.axis_size("tier"), colours)
    plan = shifts + early + far + swaps + others
    mats = rho.shape[0]
    me = lax.axis_index("tier").astype(jnp.int32)[None]
    left_fields = jnp.transpose(left_rows, (2, 1, 0))
    left_root = jnp.sqrt(left_fields[4].astype(F32))
    match_root = jnp.sqrt(match_edges[0, :, :, 4].astype(F32))
    tables = (me, left_fields, left_count, match_edges, left_root, match_root, bath_coef.T)

    first_tables = (tables[0], tables[1], tables[3])
    scalars = tables_call(plan, pairs, mats, tables)

    def size(group):
        return sum(payload(e, pairs) for e in group)

    def gather(sends, acc, scale, packs, groups):
        arrived = {e: e.permute(s) for e, s in zip(plan, sends)}
        for group in groups:
            sent = packs if group is groups[-1] else []
            offsets = [size(plan[: plan.index(e)]) for e in group]
            got = [arrived[e] for e in group]
            acc, *out = rows_call(group, sent, pairs, offsets, scale, scalars, couplings, got, acc)
        return acc, out

    rest = plan[len(shifts) :]
    pack = functools.partial(first_pack_kernel, shifts, pairs, mats)
    sends = pack_call(pack, shifts, pairs, LARGE_GRANT, first_tables, rho, in_vmem=True)
    pack = functools.partial(first_pack_kernel, rest, pairs, mats)
    sends += pack_call(pack, rest, pairs, GRANT, first_tables, rho)
    groups = [group for group in (shifts + early, swaps, far + others) if group]
    first, sends = gather(sends, local_call(damping, hamiltonian, rho), 1.0, shifts, groups)

    pack = functools.partial(next_pack_kernel, rest, pairs, size(shifts))
    sends += pack_call(pack, rest, pairs, GRANT, scalars[:1], first)
    groups = [group for group in (shifts + early, far, swaps + others) if group]
    return gather(sends, local_call(damping, hamiltonian, first, rho), 0.5 * STEP * STEP, [], groups)[0]


def solution(mesh):
    placed = (
        P(("groups", "tier"), None, None, None),
        P(),
        P(),
        P("groups", None),
        P(("groups", "tier")),
        P("tier", None, None, None),
        P(),
        P(),
    )
    return jax.shard_map(
        body,
        mesh=mesh,
        in_specs=placed,
        out_specs=P(("groups", "tier"), None, None, None),
        check_vma=False,
    )
```

```python
import functools

import jax
import jax.numpy as jnp
from jax import lax
from jax.experimental import pallas as pl
from jax.experimental.pallas import tpu as pltpu
from jax.sharding import PartitionSpec as P

REACH = 4
STEP = 0.1
F32, BF16 = jnp.float32, jnp.bfloat16
SMEM = pl.BlockSpec(memory_space=pltpu.SMEM)
HBM = pl.BlockSpec(memory_space=pltpu.HBM)
ANY = pl.BlockSpec(memory_space=pl.ANY)
GRANT, LARGE_GRANT = 24 * 1024 * 1024, 56 * 1024 * 1024


class Exchange:
    def __init__(self, kind, step, size, colour=None, listed=True):
        self.kind, self.step, self.size, self.colour, self.listed = kind, step, size, colour, listed

    def peer(self, index, outgoing):
        size, step = self.size, self.step
        if self.kind == "swap":
            return index ^ step
        if self.kind == "other":
            lower = (index & step) == 0
            if isinstance(index, int):
                return (index + (-step if lower else step)) % size
            return lax.rem(index + jnp.where(lower, size - step, step), size)
        move = step if outgoing else size - step
        if isinstance(index, int):
            return (index + move) % size
        return lax.rem(index + move, size)

    def permute(self, value):
        return lax.ppermute(value, "tier", [(i, self.peer(i, True)) for i in range(self.size)])


def exchanges(size, colours):
    shifts, short, swaps, far, others = [], [], [], [], []
    for distance in range(1, REACH + 1):
        colour = distance.bit_length() - 1
        if distance != 1 << colour or colour >= colours:
            shifts += [Exchange("shift", distance, size), Exchange("shift", size - distance, size)]
            continue
        swaps.append(Exchange("swap", distance, size, colour))
        other = Exchange("other", distance, size)
        if distance == REACH:
            others.append(other)
        else:
            short.insert(0, other)
    for colour in range(colours):
        if 1 << colour > REACH:
            far.append(Exchange("swap", 1 << colour, size, colour, listed=False))
    return shifts, short + swaps[:1], far, swaps[1:], others


def payload(exchange, pairs):
    return (pairs if exchange.colour is not None else 0) + (1 if exchange.listed else 0)


def when(condition, action):
    if condition is None:
        action()
    else:
        pl.when(condition)(action)


def split(value):
    high = value.astype(BF16)
    return high, (value - high.astype(F32)).astype(BF16)


def product(left, right):
    dot = functools.partial(jnp.dot, preferred_element_type=F32)
    return dot(left[0], right[0]) + (dot(left[0], right[1]) + dot(left[1], right[0]))


def outgoing_slots(exchange, me, mats, left_ref, match_ref):
    slots = []
    if exchange.colour is not None:
        for j in range(match_ref.shape[2]):
            slots.append(match_ref[0, exchange.colour, j, 0])
    if exchange.listed:
        peer = exchange.peer(me, True)
        slot = jnp.int32(0)
        for j in reversed(range(left_ref.shape[1])):
            source = left_ref[1, j, peer]
            slot = jnp.where(lax.div(source, mats) == me, lax.rem(source, mats), slot)
        slots.append(slot)
    return slots


def incoming_rows(exchange, me, mats, left_ref, count_ref, match_ref, left_root, match_root, bath_ref):
    rows = []

    def row(live, target, mode, flag, root):
        lower = flag == 1
        a = jnp.where(lower, jnp.float32(1), bath_ref[0, mode])
        b = jnp.where(lower, jnp.float32(0), bath_ref[1, mode])
        rows.append((live, target, mode, a * root, b * root))

    if exchange.colour is not None:
        c = exchange.colour
        for j in range(match_ref.shape[2]):
            row(None, match_ref[0, c, j, 0], match_ref[0, c, j, 2], match_ref[0, c, j, 3], match_root[c, j])
    if exchange.listed:
        peer = exchange.peer(me, False)
        found = [jnp.int32(0)] * 4 + [jnp.float32(0)]
        for j in range(left_ref.shape[1]):
            hit = (j < count_ref[me]) & (lax.div(left_ref[1, j, me], mats) == peer)
            here = [1, left_ref[0, j, me], left_ref[2, j, me], left_ref[3, j, me], left_root[j, me]]
            found = [jnp.where(hit, new, old) for new, old in zip(here, found)]
        row(found[0] == 1, found[1], found[2], found[3], found[4])
    return rows


def tables_kernel(plan, mats, me_ref, left_ref, count_ref, match_ref, left_root, match_root, bath_ref, whole, real):
    at = 0
    for exchange in plan:
        me = me_ref[0]
        slots = outgoing_slots(exchange, me, mats, left_ref, match_ref)
        rows = incoming_rows(exchange, me, mats, left_ref, count_ref, match_ref, left_root, match_root, bath_ref)
        for slot, (live, target, mode, a, b) in zip(slots, rows):
            whole[at, 0] = jnp.int32(1) if live is None else live.astype(jnp.int32)
            whole[at, 1], whole[at, 2], whole[at, 3] = target, mode, slot
            real[at, 0], real[at, 1] = a, b
            for field in range(4):
                real[at, 2 + field] = whole[at, field].astype(F32)
            at += 1


def tables_call(plan, pairs, mats, tables):
    count = sum(payload(e, pairs) for e in plan)
    return pl.pallas_call(
        functools.partial(tables_kernel, plan, mats),
        in_specs=[SMEM] * 7,
        out_specs=[SMEM] * 2,
        out_shape=[jax.ShapeDtypeStruct((count, 4), jnp.int32), jax.ShapeDtypeStruct((count, 6), F32)],
        compiler_params=pltpu.CompilerParams(vmem_limit_bytes=GRANT),
    )(*tables)


def copy_slots(slots, source, sends, sems, load_sems=None, held=None):
    loads, stores = [], []
    for at, (slot, (send, place)) in enumerate(zip(slots, sends)):
        if held is None:
            stores.append(pltpu.make_async_copy(source.at[slot], send.at[place], sems.at[at]))
            continue
        loads.append(pltpu.make_async_copy(source.at[slot], held.at[at], load_sems.at[at]))
        stores.append(pltpu.make_async_copy(held.at[at], send.at[place], sems.at[at]))
    for load in loads:
        load.start()
    for at, store in enumerate(stores):
        if loads:
            loads[at].wait()
        store.start()
    for store in stores:
        store.wait()


def places(plan, pairs, sends):
    return [(send, place) for e, send in zip(plan, sends) for place in range(payload(e, pairs))]


def first_pack_kernel(plan, pairs, mats, me_ref, left_ref, match_ref, source, *rest):
    slots = []
    for exchange in plan:
        slots += outgoing_slots(exchange, me_ref[0], mats, left_ref, match_ref)
    copy_slots(slots, source, places(plan, pairs, rest[: len(plan)]), *rest[len(plan) :])


def next_pack_kernel(plan, pairs, offset, whole, source, *rest):
    sends = places(plan, pairs, rest[: len(plan)])
    copy_slots([whole[offset + at, 3] for at in range(len(sends))], source, sends, *rest[len(plan) :])


def pack_call(kernel, plan, pairs, grant, scalars, source, in_vmem=False):
    order = source.shape[-1]
    sent = sum(payload(e, pairs) for e in plan)
    buffer = pltpu.VMEM if in_vmem else jax.ShapeDtypeStruct
    scratch = [pltpu.SemaphoreType.DMA((sent,))]
    if not in_vmem:
        scratch += [pltpu.SemaphoreType.DMA((sent,)), pltpu.VMEM((sent, 2, order, order), F32)]
    return list(
        pl.pallas_call(
            kernel,
            in_specs=[SMEM] * len(scalars) + [HBM],
            out_specs=[pl.BlockSpec(memory_space=pltpu.VMEM) if in_vmem else HBM] * len(plan),
            out_shape=[buffer((payload(e, pairs), 2, order, order), F32) for e in plan],
            scratch_shapes=scratch,
            compiler_params=pltpu.CompilerParams(vmem_limit_bytes=grant),
            cost_estimate=pl.CostEstimate(flops=0, bytes_accessed=sent * 16 * order**2, transcendentals=0),
        )(*scalars, source)
    )


def commutator(density, hamiltonian):
    parts = []
    for part in (density[0], density[1]):
        halves = split(part)
        parts.append(product(hamiltonian, halves) - product(halves, hamiltonian))
    return parts[1], -parts[0]


def local_kernel(second, damping_ref, hamiltonian_ref, density_ref, *refs):
    out_ref = refs[-1]
    decay = damping_ref[pl.program_id(0)]
    density = (density_ref[0, 0], density_ref[0, 1])
    turned = commutator(density, split(hamiltonian_ref[...]))
    for part in range(2):
        slope = turned[part] - decay * density[part]
        if second:
            slope = refs[0][0, part] + STEP * density[part] + (0.5 * STEP * STEP) * slope
        out_ref[0, part] = slope


def local_call(damping, hamiltonian, *densities):
    mats, _, order, _ = densities[0].shape
    block = pl.BlockSpec((1, 2, order, order), lambda n: (n, 0, 0, 0))
    return pl.pallas_call(
        functools.partial(local_kernel, len(densities) == 2),
        grid=(mats,),
        in_specs=[SMEM, pl.BlockSpec((order, order), lambda n: (0, 0))] + [block] * len(densities),
        out_specs=block,
        out_shape=jax.ShapeDtypeStruct(densities[0].shape, F32),
        compiler_params=pltpu.CompilerParams(vmem_limit_bytes=GRANT),
        cost_estimate=pl.CostEstimate(
            flops=mats * 24 * order**3, bytes_accessed=mats * (1 + len(densities)) * 8 * order**2, transcendentals=0
        ),
    )(damping, hamiltonian, *densities)


def rows_kernel(plan, packs, pairs, offsets, scale, real, couplings_ref, *refs):
    arrivals = refs[: len(plan)]

    def whole(index, field):
        return real[index, 2 + field].astype(jnp.int32)

    acc_in = refs[len(plan)]
    rest = refs[len(plan) + 1 :]
    acc_out, sends = rest[0], rest[1 : 1 + len(packs)]
    acc, landed, chosen, acc_sems, land_sems, mode_sems, send_sems = rest[1 + len(packs) :]
    mats = acc.shape[0]
    rows, lands, modes = [], [], []
    for exchange, offset, arrival in zip(plan, offsets, arrivals):
        for place in range(payload(exchange, pairs)):
            at = len(rows)
            index = offset + place
            live = whole(index, 0) == 1 if exchange.listed and place == payload(exchange, pairs) - 1 else None
            row = (live, whole(index, 1), whole(index, 2), real[index, 0], real[index, 1])
            lands.append(pltpu.make_async_copy(arrival.at[place], landed.at[at], land_sems.at[at]))
            modes.append(pltpu.make_async_copy(couplings_ref.at[row[2]], chosen.at[at], mode_sems.at[at]))
            rows.append(row)
    for (live, *_), land, mode in zip(rows, lands, modes):
        when(live, land.start)
        when(live, mode.start)

    def touches(n):
        return functools.reduce(
            jnp.logical_or, [row[1] == n if row[0] is None else row[0] & (row[1] == n) for row in rows]
        )

    touched = [touches(n) for n in range(mats)]
    loads = [pltpu.make_async_copy(acc_in.at[n], acc.at[n], acc_sems.at[n]) for n in range(mats)]
    stores = [pltpu.make_async_copy(acc.at[n], acc_out.at[n], acc_sems.at[n]) for n in range(mats)]
    for n in range(mats):
        when(None if packs else touched[n], loads[n].start)

    def loaded():
        for n in range(mats):
            when(None if packs else touched[n], loads[n].wait)
        for untouched, copy in early:
            when(untouched, copy.start)

    early, late, copies = [], [], []
    for at, (send, place) in enumerate(places(packs, pairs, sends)):
        slot = whole(at, 3)
        copy = pltpu.make_async_copy(acc.at[slot], send.at[place], send_sems.at[at])
        busy = touches(slot)
        copies.append(copy)
        late.append((busy, copy))
        early.append((jnp.logical_not(busy), copy))
    if rows[0][0] is not None:
        loaded()
    for at, (live, target, _, a, b) in enumerate(rows):

        def add(at=at, target=target, a=a, b=b, first=at == 0 and live is None):
            modes[at].wait()
            lands[at].wait()
            coupling = split(chosen[at])
            real, imag = split(landed[at, 0]), split(landed[at, 1])
            left_re, right_re = product(coupling, real), product(real, coupling)
            left_im, right_im = product(coupling, imag), product(imag, coupling)
            edge_re = a * (left_re - right_re) - b * (left_im + right_im)
            edge_im = a * (left_im - right_im) + b * (left_re + right_re)
            if first:
                loaded()
            acc[target, 0] += scale * edge_im
            acc[target, 1] -= scale * edge_re

        when(live, add)
    for busy, copy in late:
        when(busy, copy.start)
    for n in range(mats):
        when(touched[n], stores[n].start)
    for copy in copies:
        copy.wait()
    for n in range(mats):
        when(touched[n], stores[n].wait)


def rows_call(plan, packs, pairs, offsets, scale, scalars, couplings, arrivals, acc):
    mats, _, order, _ = acc.shape
    count = sum(payload(e, pairs) for e in plan)
    sent = sum(payload(e, pairs) for e in packs)
    shapes = [jax.ShapeDtypeStruct(acc.shape, F32)]
    shapes += [jax.ShapeDtypeStruct((payload(e, pairs), 2, order, order), F32) for e in packs]
    return pl.pallas_call(
        functools.partial(rows_kernel, plan, packs, pairs, offsets, scale),
        in_specs=[SMEM] + [HBM] + [ANY] * len(plan) + [HBM],
        out_specs=[HBM] * len(shapes),
        out_shape=shapes,
        input_output_aliases={2 + len(plan): 0},
        scratch_shapes=[
            pltpu.VMEM((mats, 2, order, order), F32),
            pltpu.VMEM((count, 2, order, order), F32),
            pltpu.VMEM((count, order, order), F32),
            pltpu.SemaphoreType.DMA((mats,)),
            pltpu.SemaphoreType.DMA((count,)),
            pltpu.SemaphoreType.DMA((count,)),
            pltpu.SemaphoreType.DMA((max(sent, 1),)),
        ],
        compiler_params=pltpu.CompilerParams(vmem_limit_bytes=GRANT),
        cost_estimate=pl.CostEstimate(flops=0, bytes_accessed=0, transcendentals=0),
    )(scalars[1], couplings, *arrivals, acc)


def body(rho, hamiltonian, couplings, bath_coef, damping, match_edges, left_rows, left_count):
    colours, pairs = match_edges.shape[1:3]
    shifts, early, far, swaps, others = exchanges(lax.axis_size("tier"), colours)
    plan = shifts + early + far + swaps + others
    mats = rho.shape[0]
    me = lax.axis_index("tier").astype(jnp.int32)[None]
    left_fields = jnp.transpose(left_rows, (2, 1, 0))
    left_root = jnp.sqrt(left_fields[4].astype(F32))
    match_root = jnp.sqrt(match_edges[0, :, :, 4].astype(F32))
    tables = (me, left_fields, left_count, match_edges, left_root, match_root, bath_coef.T)

    first_tables = (tables[0], tables[1], tables[3])
    scalars = tables_call(plan, pairs, mats, tables)

    def size(group):
        return sum(payload(e, pairs) for e in group)

    def gather(sends, acc, scale, packs, groups):
        arrived = {e: e.permute(s) for e, s in zip(plan, sends)}
        for group in groups:
            sent = packs if group is groups[-1] else []
            offsets = [size(plan[: plan.index(e)]) for e in group]
            got = [arrived[e] for e in group]
            acc, *out = rows_call(group, sent, pairs, offsets, scale, scalars, couplings, got, acc)
        return acc, out

    rest = plan[len(shifts) :]
    pack = functools.partial(first_pack_kernel, shifts, pairs, mats)
    sends = pack_call(pack, shifts, pairs, LARGE_GRANT, first_tables, rho, in_vmem=True)
    pack = functools.partial(first_pack_kernel, rest, pairs, mats)
    sends += pack_call(pack, rest, pairs, GRANT, first_tables, rho)
    groups = [group for group in (shifts + early, swaps, far + others) if group]
    first, sends = gather(sends, local_call(damping, hamiltonian, rho), 1.0, shifts, groups)

    pack = functools.partial(next_pack_kernel, rest, pairs, size(shifts))
    sends += pack_call(pack, rest, pairs, GRANT, scalars[:1], first)
    groups = [group for group in (shifts + early, far, swaps + others) if group]
    return gather(sends, local_call(damping, hamiltonian, first, rho), 0.5 * STEP * STEP, [], groups)[0]


def solution(mesh):
    placed = (
        P(("groups", "tier"), None, None, None),
        P(),
        P(),
        P("groups", None),
        P(("groups", "tier")),
        P("tier", None, None, None),
        P(),
        P(),
    )
    return jax.shard_map(
        body,
        mesh=mesh,
        in_specs=placed,
        out_specs=P(("groups", "tier"), None, None, None),
        check_vma=False,
    )
```
